32 devices in a mesh: island: 2 (over y), fsdp: 4 (over z), tensor: 4 (over x, core).
Axes of the slice: x: 2, y: 2, z: 4, core: 2. Of those that a mesh axis runs over, the one named last changes fastest.
Arguments:
- tokens: bfloat16 [1024, 6144], P(('island', 'fsdp')), may hold values from -6 to 6
- key_weight: bfloat16 [2, 6144, 1024], P('island', 'fsdp', 'tensor'), may hold values from -0.078125 to 0.078125
- key_cotangent: bfloat16 [1024, 1024], P(('island', 'fsdp'), 'tensor'), may hold values from -6 to 6
- local_frag: bfloat16 [2, 2, 6144, 2048], P('island', None, 'fsdp', 'tensor'), may hold values from -6 to 6
- outer_frag: float32 [2, 6144, 2048], P(None, 'fsdp', 'tensor'), may hold values from -6 to 6
- momentum: float32 [2, 6144, 2048], P(None, 'fsdp', 'tensor'), may hold values from -6 to 6
Outputs:
- keys: bfloat16 [1024, 1024], P(('island', 'fsdp'), 'tensor')
- input_grad: bfloat16 [1024, 6144], P(('island', 'fsdp', 'tensor'))
- weight_grad: bfloat16 [2, 6144, 1024], P('island', 'fsdp', 'tensor')
- new_outer: float32 [2, 6144, 2048], P(None, 'fsdp', 'tensor')
- new_momentum: float32 [2, 6144, 2048], P(None, 'fsdp', 'tensor')
The draws below stay inside these ranges and needn't reach their ends.
All inputs are finite; a program needn't handle non-finite values.
Results may differ from the reference program's by a relative error of at most 0.015.
Values may be sent and summed in bfloat16 or wider, within the bound.
No kernel may reach another device: no remote copies, remote signals or barrier semaphores. Data moves between devices by JAX's collectives and lax.ppermute only.
A program may use at most 128 MiB of HBM per device.

```python
import jax
import jax.numpy as jnp
from jax import lax

D = 6144
KVW = 1024
FRAG_LAYERS = 2
TOK_DEV = 128
TOKENS = 1024
N_ISLAND = 2
N_FSDP = 4
N_TENSOR = 4


def shard_levels(stream_key, dims, cuts, low, top_value):
    def one(position, blocks):
        heights = jax.random.uniform(jax.random.fold_in(jax.random.fold_in(stream_key, 6), position), (blocks,), jnp.float32, low / len(cuts), top_value / len(cuts))
        return jnp.repeat(jnp.exp(heights), dims[position] // blocks).reshape((-1,) + (1,) * (len(dims) - position - 1))

    factor_of = one(*cuts[0])
    for cut in cuts[1:]:
        factor_of = factor_of * one(*cut)
    return factor_of


def normal_values(stream_key, dims, deviation, limit, split=(), kind=jnp.bfloat16):
    drawn = jax.random.normal(stream_key, dims, jnp.float32) * deviation
    if len(split) > 0:
        drawn = shard_levels(stream_key, dims, split, -0.22, 0.18) * drawn
    return jnp.clip(drawn, min=-limit, max=limit).astype(kind)


def setup_inputs(seed: int = 0) -> dict:
    seeds = jax.random.split(jax.random.key(seed), 7)
    tokens = normal_values(seeds[0], (TOKENS, D), 1.0, 6.0, ((0, 8),))
    key_weight = normal_values(seeds[1], (N_ISLAND, D, KVW), D ** -0.5, 0.078125, ((0, 2), (1, 4), (2, 4)))
    key_cotangent = normal_values(seeds[2], (TOKENS, KVW), 1.0, 6.0, ((0, 8), (1, 4)))
    local_frag = normal_values(seeds[3], (N_ISLAND, FRAG_LAYERS, D, 2 * KVW), 1.0, 6.0, ((0, 2), (2, 4), (3, 4)))
    outer_frag = normal_values(seeds[4], (FRAG_LAYERS, D, 2 * KVW), 1.0, 6.0, ((1, 4), (2, 4)), jnp.float32)
    momentum = normal_values(seeds[5], (FRAG_LAYERS, D, 2 * KVW), 1.0, 6.0, ((1, 4), (2, 4)), jnp.float32)
    return {"tokens": tokens, "key_weight": key_weight, "key_cotangent": key_cotangent, "local_frag": local_frag, "outer_frag": outer_frag, "momentum": momentum}


outer_rate = 0.7
beta_outer = 0.9


def island_work(bundle):
    tok_block, weight_block, cotangent_block = bundle
    keys = jnp.dot(tok_block, weight_block, preferred_element_type=jnp.float32).astype(jnp.bfloat16)
    head_cols = KVW // N_TENSOR
    input_sum = jnp.zeros((tok_block.shape[0], D), jnp.float32)
    for member in range(N_TENSOR):
        grad_part = jnp.dot(cotangent_block[:, member * head_cols:(member + 1) * head_cols],
                            weight_block[:, member * head_cols:(member + 1) * head_cols].T,
                            preferred_element_type=jnp.float32)
        input_sum = input_sum + grad_part.astype(jnp.bfloat16).astype(jnp.float32)
    weight_sum = jnp.zeros((D, KVW), jnp.float32)
    for member in range(N_FSDP):
        tok_rows = tok_block[member * TOK_DEV:(member + 1) * TOK_DEV]
        cot_rows = cotangent_block[member * TOK_DEV:(member + 1) * TOK_DEV]
        grad_part = jnp.dot(tok_rows.T, cot_rows, preferred_element_type=jnp.float32)
        weight_sum = weight_sum + grad_part.astype(jnp.bfloat16).astype(jnp.float32)
    return keys, input_sum.astype(jnp.bfloat16), weight_sum.astype(jnp.bfloat16)


def reference(tokens, key_weight, key_cotangent, local_frag, outer_frag, momentum):
    island_rows = TOK_DEV * N_FSDP
    tok_all = tokens.reshape(N_ISLAND, island_rows, D)
    cot_all = key_cotangent.reshape(N_ISLAND, island_rows, KVW)
    keys, input_grad, weight_grad = lax.map(island_work, (tok_all, key_weight, cot_all))
    frag_sum = jnp.zeros(outer_frag.shape, jnp.float32)
    for member in range(N_ISLAND):
        frag_sum = frag_sum + local_frag[member].astype(jnp.float32)
    average = outer_frag - frag_sum / N_ISLAND
    new_momentum = beta_outer * momentum + average
    new_outer = outer_frag - outer_rate * (average + beta_outer * new_momentum)
    return (keys.reshape(N_ISLAND * island_rows, KVW), input_grad.reshape(N_ISLAND * island_rows, D),
            weight_grad, new_outer, new_momentum)
```

```python
import functools

import jax
import jax.numpy as jnp
from jax import lax
from jax.experimental import pallas as pl
from jax.experimental.pallas import tpu as pltpu
from jax.sharding import PartitionSpec as P

outer_rate = 0.7
beta_outer = 0.9
F32 = jnp.float32
BF16 = jnp.bfloat16


def nesterov(frag_sum, outer, momentum, islands):
    average = outer - frag_sum / islands
    new_momentum = beta_outer * momentum + average
    return outer - outer_rate * (average + beta_outer * new_momentum), new_momentum


def update_kernel(islands, theirs, ours, outer, momentum, *refs):
    new_outer, new_momentum = refs[-2:]
    frag_sum = ours[...].astype(F32) + theirs[...].astype(F32)
    new_outer[...], new_momentum[...] = nesterov(frag_sum, outer[...], momentum[...], islands)


def update_chunk(theirs, ours, outer, momentum, done, first, block, islands):
    rows, cols = theirs.shape
    here = pl.BlockSpec((block, cols), lambda i: (i, 0))
    there = pl.BlockSpec((block, cols), lambda i: (i + first // block, 0))
    kept = [pl.BlockSpec(memory_space=pl.ANY)] * len(done)
    return pl.pallas_call(
        functools.partial(update_kernel, islands),
        grid=(rows // block,),
        in_specs=[here, there, there, there] + kept,
        out_specs=[there, there],
        out_shape=[jax.ShapeDtypeStruct(outer.shape, F32)] * 2,
        input_output_aliases={4 + i: i for i in range(len(done))},
        cost_estimate=pl.CostEstimate(flops=10 * rows * cols, bytes_accessed=20 * rows * cols, transcendentals=0),
    )(theirs, ours, outer, momentum, *done)


def outer_step(local_frag, outer_frag, momentum):
    islands = lax.axis_size("island")
    if islands != 2:
        return nesterov(lax.psum(local_frag[0], "island").astype(F32), outer_frag, momentum, islands)
    cols = local_frag.shape[-1]
    ours, outer, held = (a.reshape(-1, cols) for a in (local_frag, outer_frag, momentum))
    units = 16
    block = ours.shape[0] // units
    sizes = [1, 2, 2, 2, 2, 2, 2, 2, 1]
    starts = [sum(sizes[:k]) * block for k in range(len(sizes))]
    swap = [(0, 1), (1, 0)]
    source = ours
    arrived = []
    for size, first in zip(sizes, starts):
        piece = lax.slice_in_dim(source, first, first + size * block)
        if first == 0:
            piece, source = lax.optimization_barrier((piece, source))
        arrived.append(lax.ppermute(piece, "island", swap))
    done = ()
    for theirs, first in zip(arrived, starts):
        done = update_chunk(theirs, ours, outer, held, done, first, block, islands)
    return tuple(a.reshape(outer_frag.shape) for a in done)


def shifted(x, axis, step):
    n = lax.axis_size(axis)
    return lax.ppermute(x, axis, [(i, (i + step) % n) for i in range(n)])


def sum_scatter(part_of, axis):
    n = lax.axis_size(axis)
    if n & (n - 1):
        me = lax.axis_index(axis)
        stacked = jnp.concatenate([part_of([lax.rem(me + k, n)])[None] for k in range(n)]).astype(BF16)
        return lax.psum_scatter(jnp.roll(stacked, me, axis=0), axis, scatter_dimension=0)[0].astype(F32)
    me = lax.axis_index(axis)
    received = {k: [] for k in range(n)}
    bit = 1
    while bit < n:
        leaving = [k for k in range(bit, n, 2 * bit)]
        part = part_of([me ^ k for k in leaving])
        if any(received[k] for k in leaving):
            part = part + sum(jnp.concatenate(r) for r in zip(*(received[k] for k in leaving)))
        came = lax.ppermute(part.astype(BF16), axis, [(i, i ^ bit) for i in range(n)])
        for slot, block in zip(leaving, jnp.split(came.astype(F32), len(leaving))):
            received[slot ^ bit].append(block)
        bit *= 2
    return part_of([me]) + sum(received[0])


def projection_step(tokens, weight, cotangent):
    shards, heads = lax.axis_size("fsdp"), lax.axis_size("tensor")
    me = lax.axis_index("fsdp")
    width = weight.shape[0]
    rows = tokens.shape[0]
    cots = [cotangent] + [shifted(cotangent, "fsdp", s) for s in range(1, shards)]
    toks = []
    for s in range(shards):
        piece = lax.dynamic_slice_in_dim(tokens, lax.rem(me + s, shards) * width, width, 1)
        toks.append(shifted(piece, "fsdp", s) if s else piece)

    share = rows // heads
    all_cots = jnp.stack(cots)

    def part_of(members):
        mine = jnp.concatenate([lax.dynamic_slice_in_dim(all_cots, m * share, share, 1) for m in members])
        return lax.dot_general(mine.reshape(-1, mine.shape[-1]), weight, (((1,), (1,)), ((), ())), preferred_element_type=F32)

    summed = sum_scatter(part_of, "tensor").astype(BF16).reshape(shards, share, width)
    pieces = [summed[0]] + [shifted(summed[s], "fsdp", -s) for s in range(1, shards)]
    input_grad = jnp.roll(jnp.concatenate(pieces, axis=1), me * width, axis=1)

    weight_grad = lax.dot_general(
        jnp.concatenate(toks), jnp.concatenate(cots), (((0,), (0,)), ((), ())), preferred_element_type=F32
    ).astype(BF16)

    keys = jnp.dot(toks[0], weight, preferred_element_type=F32)
    for s in range(1, shards):
        part = jnp.dot(toks[s], weight, preferred_element_type=F32).astype(BF16)
        keys = keys + shifted(part, "fsdp", -s).astype(F32)
    return keys.astype(BF16), input_grad, weight_grad


def body(tokens, key_weight, key_cotangent, local_frag, outer_frag, momentum):
    new_outer, new_momentum = outer_step(local_frag, outer_frag, momentum)
    keys, input_grad, weight_grad = projection_step(tokens, key_weight[0], key_cotangent)
    return (keys, input_grad, weight_grad[None], new_outer, new_momentum)


def solution(mesh):
    return jax.shard_map(
        body,
        mesh=mesh,
        in_specs=(
            P(("island", "fsdp"), None),
            P("island", "fsdp", "tensor"),
            P(("island", "fsdp"), "tensor"),
            P("island", None, "fsdp", "tensor"),
            P(None, "fsdp", "tensor"),
            P(None, "fsdp", "tensor"),
        ),
        out_specs=(
            P(("island", "fsdp"), "tensor"),
            P(("island", "fsdp", "tensor"), None),
            P("island", "fsdp", "tensor"),
            P(None, "fsdp", "tensor"),
            P(None, "fsdp", "tensor"),
        ),
        check_vma=False,
    )
```

```python
import functools

import jax
import jax.numpy as jnp
from jax import lax
from jax.experimental import pallas as pl
from jax.experimental.pallas import tpu as pltpu
from jax.sharding import PartitionSpec as P

outer_rate = 0.7
beta_outer = 0.9
F32 = jnp.float32
BF16 = jnp.bfloat16
units = 32
chunk_units = ((0, 9), (9, 11), (20, 9), (29, 3))


def nesterov(frag_sum, outer, momentum, islands):
    average = outer - frag_sum / islands
    new_momentum = beta_outer * momentum + average
    return outer - outer_rate * (average + beta_outer * new_momentum), new_momentum


def unwritten(like):
    return pl.pallas_call(
        lambda *_: None,
        out_specs=[pl.BlockSpec(memory_space=pltpu.HBM)] * 2,
        out_shape=[jax.ShapeDtypeStruct(like.shape, like.dtype)] * 2,
        cost_estimate=pl.CostEstimate(flops=0, bytes_accessed=0, transcendentals=0),
    )()


def update(k, theirs, local_frag, outer_frag, momentum, done):
    ours, outer, held = (a.reshape(-1, a.shape[-1]) for a in (local_frag, outer_frag, momentum))
    if done is None:
        done = unwritten(outer)
    first = chunk_units[k][0] * (ours.shape[0] // units)
    ours, outer, held = (lax.slice_in_dim(a, first, first + theirs.shape[0]) for a in (ours, outer, held))
    results = nesterov(ours.astype(F32) + theirs.astype(F32), outer, held, lax.axis_size("island"))
    return [lax.dynamic_update_slice(whole, part, (first, 0)) for whole, part in zip(done, results)]


def piece_kernel(firsts, ours, *refs):
    pieces, buffers, loads, stores = refs[: len(firsts)], refs[len(firsts) : -2], refs[-2], refs[-1]
    inward = [
        pltpu.make_async_copy(ours.at[pl.ds(first, piece.shape[0])], buffer, loads.at[k])
        for k, (first, piece, buffer) in enumerate(zip(firsts, pieces, buffers))
    ]
    outward = [pltpu.make_async_copy(buffer, piece, stores.at[k]) for k, (piece, buffer) in enumerate(zip(pieces, buffers))]
    for copy in inward:
        copy.start()
    for load, store in zip(inward, outward):
        load.wait()
        store.start()
    for copy in outward:
        copy.wait()


def pieces_of(local_frag, members):
    ours = local_frag.reshape(-1, local_frag.shape[-1])
    unit, cols = ours.shape[0] // units, ours.shape[1]
    firsts = [chunk_units[k][0] * unit for k in members]
    shapes = [(chunk_units[k][1] * unit, cols) for k in members]
    return pl.pallas_call(
        functools.partial(piece_kernel, firsts),
        in_specs=[pl.BlockSpec(memory_space=pltpu.HBM)],
        out_specs=[pl.BlockSpec(memory_space=pltpu.HBM)] * len(members),
        out_shape=[jax.ShapeDtypeStruct(s, BF16) for s in shapes],
        scratch_shapes=[pltpu.VMEM(s, BF16) for s in shapes] + [pltpu.SemaphoreType.DMA((len(members),))] * 2,
        compiler_params=pltpu.CompilerParams(vmem_limit_bytes=16 * 1024 * 1024),
        cost_estimate=pl.CostEstimate(flops=0, bytes_accessed=0, transcendentals=0),
    )(ours)


def swapped(piece):
    return lax.ppermute(piece, "island", [(0, 1), (1, 0)])


def together(f, *operands):
    shapes = jax.eval_shape(f, *operands)
    return lax.cond(
        lax.axis_index("fsdp") >= 0, f, lambda *_: jax.tree.map(lambda s: jnp.zeros(s.shape, s.dtype), shapes), *operands
    )


def shifted(x, axis, step):
    n = lax.axis_size(axis)
    return lax.ppermute(x, axis, [(i, (i + step) % n) for i in range(n)])


def paired(x, axis, bit):
    return lax.ppermute(x, axis, [(i, i ^ bit) for i in range(lax.axis_size(axis))])


def leaving_at(axis, bit):
    return [lax.axis_index(axis) ^ k for k in range(bit, lax.axis_size(axis), 2 * bit)]


def input_terms(cots, weight):
    share = cots.shape[1] // lax.axis_size("tensor")

    def part_of(members):
        rows_of = jnp.concatenate([lax.dynamic_slice_in_dim(cots, m * share, share, 1) for m in members])
        return lax.dot_general(
            rows_of.reshape(-1, cots.shape[2]), weight, (((1,), (1,)), ((), ())), preferred_element_type=F32
        )

    return part_of


def sum_scatter(part, part_of, axis):
    n = lax.axis_size(axis)
    received = {k: [] for k in range(n)}
    bit = 1
    while bit < n:
        leaving = list(range(bit, n, 2 * bit))
        if bit > 1:
            part = part_of(leaving_at(axis, bit))
            for terms in zip(*(received[k] for k in leaving)):
                part = part + jnp.concatenate([t.astype(F32) for t in terms])
        came = paired(part.astype(BF16), axis, bit)
        for slot, block in zip(leaving, jnp.split(came, len(leaving))):
            received[slot ^ bit].append(block)
        bit *= 2
    return part_of([lax.axis_index(axis)]) + sum(t.astype(F32) for t in received[0])


def keys_kernel(place, own, *refs):
    peers = (len(refs) - 3) // 3
    mine, other = refs[:peers], refs[peers : 2 * peers]
    weight, summed, keys_own, *packets = refs[2 * peers :]
    core = place[1]
    half, cols = own.shape[0] // 2, weight.shape[1]
    share = summed.shape[0] // (peers + 1)
    keys_own[...] = jnp.dot(own[...], weight[...], preferred_element_type=F32)
    for blocks, at in ((mine, core), (other, 1 - core)):
        for block, packet in zip(blocks, packets):
            part = jnp.dot(block[...], weight[...], preferred_element_type=F32)
            packet[pl.ds(pl.multiple_of(at * half, half), half), :] = part.astype(BF16)
    for s, packet in enumerate(packets, 1):
        for j in range(summed.shape[1] // cols):
            top = 2 * half + j * share
            packet[top : top + share, :] = summed[s * share : (s + 1) * share, j * cols : (j + 1) * cols]


def finish_kernel(place, keys_own, summed, *refs):
    packets, (keys, input_grad) = refs[:-2], refs[-2:]
    shards = len(packets) + 1
    rows, cols = keys.shape
    share, width = input_grad.shape[0], summed.shape[1]
    total = keys_own[...]
    for packet in packets:
        total = total + packet[:rows, :].astype(F32)
    keys[...] = total.astype(BF16)
    input_grad[:, pl.ds(pl.multiple_of(place[0] * width, width), width)] = summed[:share, :]
    for s, packet in enumerate(packets, 1):
        origin = lax.rem(place[0] + s, shards) * width
        for j in range(width // cols):
            top = rows + j * share
            input_grad[:, pl.ds(pl.multiple_of(origin + j * cols, cols), cols)] = packet[top : top + share, :]


def weight_grad_kernel(place, own, *refs):
    peers = (len(refs) - 2) // 2
    mine, other, (cots, weight_grad) = refs[:peers], refs[peers : 2 * peers], refs[2 * peers :]
    core = place[1]
    half = own.shape[0] // 2
    tokens, rows = [own[...]], [cots[0]]
    for blocks, at in ((mine, core), (other, 1 - core)):
        for s, block in enumerate(blocks, 1):
            tokens.append(block[...])
            rows.append(cots[s, pl.ds(pl.multiple_of(at * half, half), half), :])
    total = lax.dot_general(
        jnp.concatenate(tokens), jnp.concatenate(rows), (((0,), (0,)), ((), ())), preferred_element_type=F32
    )
    weight_grad[...] = total.astype(BF16)


def local_call(kernel, out_shape, place, tokens, *operands, flops=0):
    whole = pl.BlockSpec(memory_space=pltpu.VMEM)
    first = [] if tokens is None else [tokens]
    width = first[0].shape[1] // lax.axis_size("fsdp") if first else 0
    columns = [pl.BlockSpec((a.shape[0], width), lambda i, place: (0, place[0])) for a in first]
    return pl.pallas_call(
        kernel,
        grid_spec=pltpu.PrefetchScalarGridSpec(
            num_scalar_prefetch=1, grid=(1,), in_specs=columns + [whole] * len(operands), out_specs=[whole] * len(out_shape)
        ),
        out_shape=out_shape,
        compiler_params=pltpu.CompilerParams(vmem_limit_bytes=32 * 1024 * 1024),
        cost_estimate=pl.CostEstimate(flops=flops, bytes_accessed=0, transcendentals=0),
    )(place, *first, *operands)


def place_of():
    return lax.axis_index("fsdp"), lax.rem(lax.axis_index("tensor"), 2)


def gather(tokens, weight, cotangent):
    me, core = place_of()
    shards = lax.axis_size("fsdp")
    width, half = weight.shape[0], tokens.shape[0] // 2
    leaving = [
        lax.dynamic_slice(tokens, (core * half, lax.rem(me + s, shards) * width), (half, width)) for s in range(1, shards)
    ]
    cots = [cotangent] + [shifted(cotangent, "fsdp", s) for s in range(1, shards)]
    mine = shifted(leaving[0], "fsdp", 1)
    mine, cots = lax.optimization_barrier((mine, cots))
    cots = jnp.stack(cots)
    return cots, input_terms(cots, weight)(leaving_at("tensor", 1)).astype(BF16), mine, leaving[1:]


def combine(cots, part, mine, leaving, tokens, weight):
    place = jnp.stack(place_of()).astype(jnp.int32)
    shards, heads = lax.axis_size("fsdp"), lax.axis_size("tensor")
    width, cols = weight.shape
    rows = tokens.shape[0]
    share = rows // heads

    mine = [mine] + [shifted(block, "fsdp", s) for s, block in enumerate(leaving, 2)]
    other = [paired(block, "tensor", 1) for block in mine]
    summed = sum_scatter(part, input_terms(cots, weight), "tensor").astype(BF16)
    packet = jax.ShapeDtypeStruct((rows + share * width // cols, cols), BF16)
    keys_own, *packets = local_call(
        keys_kernel,
        [jax.ShapeDtypeStruct((rows, cols), F32)] + [packet] * (shards - 1),
        place, tokens, *mine, *other, weight, summed,
    )
    return (cots, mine, other), (keys_own, summed), packets


def finish(gathered, own, packets, tokens, weight):
    place = jnp.stack(place_of()).astype(jnp.int32)
    cots, mine, other = gathered
    keys_own, summed = own
    shards, rows, cols = cots.shape
    packets = [shifted(p, "fsdp", -s) for s, p in enumerate(packets, 1)]
    (weight_grad,) = local_call(
        weight_grad_kernel, [jax.ShapeDtypeStruct(weight.shape, BF16)], place, tokens, *mine, *other, cots
    )
    keys, input_grad = local_call(
        finish_kernel,
        [jax.ShapeDtypeStruct((rows, cols), BF16), jax.ShapeDtypeStruct((summed.shape[0] // shards, tokens.shape[1]), BF16)],
        place, None, keys_own, summed, *packets,
    )
    return keys, input_grad, weight_grad


def body(tokens, key_weight, key_cotangent, local_frag, outer_frag, momentum):
    weight = key_weight[0]
    islands = lax.axis_size("island")
    if islands != 2:
        state = combine(*gather(tokens, weight, key_cotangent), tokens, weight)
        keys, input_grad, weight_grad = finish(*state, tokens, weight)
        frag_sum = lax.psum(local_frag[0], "island").astype(F32)
        new_outer, new_momentum = nesterov(frag_sum, outer_frag, momentum, islands)
        return (keys, input_grad, weight_grad[None], new_outer, new_momentum)

    frag = (local_frag, outer_frag, momentum)
    theirs = [swapped(*pieces_of(local_frag, [0]))]

    def step_one(tokens, weight, key_cotangent, local_frag):
        return gather(tokens, weight, key_cotangent), pieces_of(local_frag, [1])

    state, (piece,) = together(step_one, tokens, weight, key_cotangent, local_frag)
    theirs.append(swapped(piece))
    theirs[0], state = lax.optimization_barrier((theirs[0], state))

    def step_two(theirs, state, tokens, weight, *frag):
        pieces = pieces_of(frag[0], range(2, len(chunk_units)))
        return combine(*state, tokens, weight), pieces, update(0, theirs, *frag, None)

    state, pieces, done = together(step_two, theirs[0], state, tokens, weight, *frag)
    theirs.append(swapped(pieces[0]))
    theirs[1], state, done = lax.optimization_barrier((theirs[1], state, done))

    def step_three(theirs, state, done, tokens, weight, *frag):
        return finish(*state, tokens, weight), update(1, theirs, *frag, done)

    (keys, input_grad, weight_grad), done = together(step_three, theirs[1], state, done, tokens, weight, *frag)
    theirs += [swapped(piece) for piece in pieces[1:]]
    for k in range(2, len(theirs)):
        theirs[k], done = lax.optimization_barrier((theirs[k], done))
        done = update(k, theirs[k], *frag, done)
    new_outer, new_momentum = (a.reshape(outer_frag.shape) for a in done)
    return (keys, input_grad, weight_grad[None], new_outer, new_momentum)


def solution(mesh):
    return jax.shard_map(
        body,
        mesh=mesh,
        in_specs=(
            P(("island", "fsdp"), None),
            P("island", "fsdp", "tensor"),
            P(("island", "fsdp"), "tensor"),
            P("island", None, "fsdp", "tensor"),
            P(None, "fsdp", "tensor"),
            P(None, "fsdp", "tensor"),
        ),
        out_specs=(
            P(("island", "fsdp"), "tensor"),
            P(("island", "fsdp", "tensor"), None),
            P("island", "fsdp", "tensor"),
            P(None, "fsdp", "tensor"),
            P(None, "fsdp", "tensor"),
        ),
        check_vma=False,
    )
```

```python
import functools

import jax
import jax.numpy as jnp
from jax import lax
from jax.experimental import pallas as pl
from jax.experimental.pallas import tpu as pltpu
from jax.sharding import PartitionSpec as P

outer_rate = 0.7
beta_outer = 0.9
F32 = jnp.float32
BF16 = jnp.bfloat16
units = 32
chunk_units = ((0, 19, 4), (19, 10, 2), (29, 3, None))


def nesterov(frag_sum, outer, momentum, islands):
    average = outer - frag_sum / islands
    new_momentum = beta_outer * momentum + average
    return outer - outer_rate * (average + beta_outer * new_momentum), new_momentum


def update_kernel(islands, first, cuts, theirs, ours, outer, momentum, *refs):
    new_outer, new_momentum, their_rows, our_rows, outer_rows, momentum_rows, loads, stores = refs[-8:]
    arriving, leaving = [], []
    for k, (top, bottom) in enumerate(zip(cuts, cuts[1:])):
        here, there = pl.ds(top, bottom - top), pl.ds(first + top, bottom - top)
        sources = (theirs.at[here], ours.at[there], outer.at[there], momentum.at[there])
        buffers = (their_rows, our_rows, outer_rows, momentum_rows)
        arriving.append([pltpu.make_async_copy(s, b.at[here], loads.at[i, k]) for i, (s, b) in enumerate(zip(sources, buffers))])
        results = ((outer_rows, new_outer), (momentum_rows, new_momentum))
        leaving.append([pltpu.make_async_copy(b.at[here], d.at[there], stores.at[i, k]) for i, (b, d) in enumerate(results)])
    for copies in arriving:
        for copy in copies:
            copy.start()
    for (top, bottom), copies, results in zip(zip(cuts, cuts[1:]), arriving, leaving):
        for copy in copies:
            copy.wait()
        rows = slice(top, bottom)
        frag_sum = our_rows[rows].astype(F32) + their_rows[rows].astype(F32)
        outer_rows[rows], momentum_rows[rows] = nesterov(frag_sum, outer_rows[rows], momentum_rows[rows], islands)
        for copy in results:
            copy.start()
    for copies in leaving:
        for copy in copies:
            copy.wait()


def update(k, theirs, local_frag, outer_frag, momentum, done):
    islands = lax.axis_size("island")
    ours, outer, held = (a.reshape(-1, a.shape[-1]) for a in (local_frag, outer_frag, momentum))
    unit = ours.shape[0] // units
    (first, size, parts), cols = chunk_units[k], ours.shape[1]
    first, rows = first * unit, size * unit
    if parts is None:
        ours, outer, held = (lax.slice_in_dim(a, first, first + rows) for a in (ours, outer, held))
        results = nesterov(ours.astype(F32) + theirs.astype(F32), outer, held, islands)
        return [lax.dynamic_update_slice(whole, part, (first, 0)) for whole, part in zip(done, results)]
    cuts = [rows * i // parts // 16 * 16 for i in range(parts)] + [rows]
    hbm = pl.BlockSpec(memory_space=pltpu.HBM)
    return pl.pallas_call(
        functools.partial(update_kernel, islands, first, cuts),
        in_specs=[hbm] * (4 + len(done)),
        out_specs=[hbm] * 2,
        out_shape=[jax.ShapeDtypeStruct(outer.shape, F32)] * 2,
        scratch_shapes=[pltpu.VMEM((rows, cols), BF16)] * 2
        + [pltpu.VMEM((rows, cols), F32)] * 2
        + [pltpu.SemaphoreType.DMA((4, parts)), pltpu.SemaphoreType.DMA((2, parts))],
        input_output_aliases={4 + i: i for i in range(len(done))},
        compiler_params=pltpu.CompilerParams(vmem_limit_bytes=32 * 1024 * 1024),
        cost_estimate=pl.CostEstimate(flops=0, bytes_accessed=0, transcendentals=0),
    )(theirs, ours, outer, held, *done)


def piece_kernel(parts, ours, *refs):
    pieces, buffers, loads, stores = refs[: len(parts)], refs[len(parts) : -2], refs[-2], refs[-1]
    inward, outward = [], []
    for (first, cuts), piece, buffer in zip(parts, pieces, buffers):
        for top, bottom in zip(cuts, cuts[1:]):
            rows, k = pl.ds(top, bottom - top), len(inward)
            inward.append(pltpu.make_async_copy(ours.at[pl.ds(first + top, bottom - top)], buffer.at[rows], loads.at[k]))
            outward.append(pltpu.make_async_copy(buffer.at[rows], piece.at[rows], stores.at[k]))
    for copy in inward:
        copy.start()
    for load, store in zip(inward, outward):
        load.wait()
        store.start()
    for copy in outward:
        copy.wait()


def pieces_of(local_frag, members, hint=0):
    ours = local_frag.reshape(-1, local_frag.shape[-1])
    unit, cols = ours.shape[0] // units, ours.shape[1]
    shapes = [(chunk_units[k][1] * unit, cols) for k in members]
    parts = []
    for k, (rows, _) in zip(members, shapes):
        cuts = list(range(0, rows, 4 * unit)) + [rows]
        parts.append((chunk_units[k][0] * unit, cuts))
    copies = sum(len(cuts) - 1 for _, cuts in parts)
    return pl.pallas_call(
        functools.partial(piece_kernel, parts),
        in_specs=[pl.BlockSpec(memory_space=pltpu.HBM)],
        out_specs=[pl.BlockSpec(memory_space=pltpu.HBM)] * len(members),
        out_shape=[jax.ShapeDtypeStruct(s, BF16) for s in shapes],
        scratch_shapes=[pltpu.VMEM(s, BF16) for s in shapes] + [pltpu.SemaphoreType.DMA((copies,))] * 2,
        compiler_params=pltpu.CompilerParams(vmem_limit_bytes=16 * 1024 * 1024),
        cost_estimate=pl.CostEstimate(flops=hint, bytes_accessed=0, transcendentals=0),
    )(ours)


def swapped(piece):
    return lax.ppermute(piece, "island", [(0, 1), (1, 0)])


def together(f, *operands):
    shapes = jax.eval_shape(f, *operands)
    return lax.cond(
        lax.axis_index("fsdp") >= 0, f, lambda *_: jax.tree.map(lambda s: jnp.zeros(s.shape, s.dtype), shapes), *operands
    )


def shifted(x, axis, step):
    n = lax.axis_size(axis)
    return lax.ppermute(x, axis, [(i, (i + step) % n) for i in range(n)])


def paired(x, axis, bit):
    return lax.ppermute(x, axis, [(i, i ^ bit) for i in range(lax.axis_size(axis))])


def leaving_at(axis, bit):
    return [lax.axis_index(axis) ^ k for k in range(bit, lax.axis_size(axis), 2 * bit)]


def input_terms(cots, weight):
    share = cots.shape[1] // lax.axis_size("tensor")

    def part_of(members):
        rows_of = jnp.concatenate([lax.dynamic_slice_in_dim(cots, m * share, share, 1) for m in members])
        return lax.dot_general(
            rows_of.reshape(-1, cots.shape[2]), weight, (((1,), (1,)), ((), ())), preferred_element_type=F32
        )

    return part_of


def sum_scatter(came, part_of, axis):
    n = lax.axis_size(axis)
    received = {k: [] for k in range(n)}
    bit = 1
    while bit < n:
        leaving = list(range(bit, n, 2 * bit))
        if bit > 1:
            part = part_of(leaving_at(axis, bit))
            for terms in zip(*(received[k] for k in leaving)):
                part = part + jnp.concatenate([t.astype(F32) for t in terms])
            came = paired(part.astype(BF16), axis, bit)
        for slot, block in zip(leaving, jnp.split(came, len(leaving))):
            received[slot ^ bit].append(block)
        bit *= 2
    return part_of([lax.axis_index(axis)]) + sum(t.astype(F32) for t in received[0])


def keys_kernel(place, own, *refs):
    peers = (len(refs) - 3) // 3
    mine, other = refs[:peers], refs[peers : 2 * peers]
    weight, summed, keys_own, *packets = refs[2 * peers :]
    core = place[1]
    half, cols = own.shape[0] // 2, weight.shape[1]
    share = summed.shape[0] // (peers + 1)
    rows = jnp.concatenate([own[...]] + [block[...] for block in (*mine, *other)])
    part = jnp.dot(rows, weight[...], preferred_element_type=F32)
    keys_own[...] = part[: 2 * half]
    part = part.astype(BF16)
    for s, packet in enumerate(packets):
        for top, at in ((2 + s) * half, core), ((2 + peers + s) * half, 1 - core):
            packet[pl.ds(pl.multiple_of(at * half, half), half), :] = part[top : top + half]
    for s, packet in enumerate(packets, 1):
        for j in range(summed.shape[1] // cols):
            top = 2 * half + j * share
            packet[top : top + share, :] = summed[s * share : (s + 1) * share, j * cols : (j + 1) * cols]


def finish_kernel(place, keys_own, summed, *refs):
    packets, (keys, input_grad) = refs[:-2], refs[-2:]
    shards = len(packets) + 1
    rows, cols = keys.shape
    share, width = input_grad.shape[0], summed.shape[1]
    total = keys_own[...]
    for packet in packets:
        total = total + packet[:rows, :].astype(F32)
    keys[...] = total.astype(BF16)
    input_grad[:, pl.ds(pl.multiple_of(place[0] * width, width), width)] = summed[:share, :]
    for s, packet in enumerate(packets, 1):
        origin = lax.rem(place[0] + s, shards) * width
        for j in range(width // cols):
            top = rows + j * share
            input_grad[:, pl.ds(pl.multiple_of(origin + j * cols, cols), cols)] = packet[top : top + share, :]


def weight_grad_kernel(place, own, *refs):
    peers = (len(refs) - 2) // 2
    mine, other, (cots, weight_grad) = refs[:peers], refs[peers : 2 * peers], refs[2 * peers :]
    core = place[1]
    half = own.shape[0] // 2
    tokens, rows = [own[...]], [cots[0]]
    for blocks, at in ((mine, core), (other, 1 - core)):
        for s, block in enumerate(blocks, 1):
            tokens.append(block[...])
            rows.append(cots[s, pl.ds(pl.multiple_of(at * half, half), half), :])
    total = lax.dot_general(
        jnp.concatenate(tokens), jnp.concatenate(rows), (((0,), (0,)), ((), ())), preferred_element_type=F32
    )
    weight_grad[...] = total.astype(BF16)


def local_call(kernel, out_shape, place, tokens, *operands, flops=0):
    whole = pl.BlockSpec(memory_space=pltpu.VMEM)
    first = [] if tokens is None else [tokens]
    width = first[0].shape[1] // lax.axis_size("fsdp") if first else 0
    columns = [pl.BlockSpec((a.shape[0], width), lambda i, place: (0, place[0])) for a in first]
    return pl.pallas_call(
        kernel,
        grid_spec=pltpu.PrefetchScalarGridSpec(
            num_scalar_prefetch=1, grid=(1,), in_specs=columns + [whole] * len(operands), out_specs=[whole] * len(out_shape)
        ),
        out_shape=out_shape,
        compiler_params=pltpu.CompilerParams(vmem_limit_bytes=32 * 1024 * 1024),
        cost_estimate=pl.CostEstimate(flops=flops, bytes_accessed=0, transcendentals=0),
    )(place, *first, *operands)


def place_of():
    return lax.axis_index("fsdp"), lax.rem(lax.axis_index("tensor"), 2)


def columns_for(tokens, s, width):
    me, core = place_of()
    half = tokens.shape[0] // 2
    return lax.dynamic_slice(tokens, (core * half, lax.rem(me + s, lax.axis_size("fsdp")) * width), (half, width))


def gather(tokens, weight, cotangent):
    cots = jnp.stack([cotangent] + [shifted(cotangent, "fsdp", s) for s in range(1, lax.axis_size("fsdp"))])
    part = input_terms(cots, weight)(leaving_at("tensor", 1)).astype(BF16)
    return cots, part, shifted(columns_for(tokens, 1, weight.shape[0]), "fsdp", 1)


def combine(cots, part, mine, tokens, weight):
    place = jnp.stack(place_of()).astype(jnp.int32)
    shards, heads = lax.axis_size("fsdp"), lax.axis_size("tensor")
    width, cols = weight.shape
    rows = tokens.shape[0]
    share = rows // heads

    part = paired(part, "tensor", 1)
    mine = [mine] + [shifted(columns_for(tokens, s, width), "fsdp", s) for s in range(2, shards)]
    other = [paired(block, "tensor", 1) for block in mine]
    summed = sum_scatter(part, input_terms(cots, weight), "tensor").astype(BF16)
    packet = jax.ShapeDtypeStruct((rows + share * width // cols, cols), BF16)
    keys_own, *packets = local_call(
        keys_kernel,
        [jax.ShapeDtypeStruct((rows, cols), F32)] + [packet] * (shards - 1),
        place, tokens, *mine, *other, weight, summed,
    )
    return mine[1:], other, (keys_own, summed), packets


def finish(cots, mine, more, other, own, packets, tokens, weight):
    place = jnp.stack(place_of()).astype(jnp.int32)
    mine = [mine, *more]
    keys_own, summed = own
    shards, rows, cols = cots.shape
    packets = [shifted(p, "fsdp", -s) for s, p in enumerate(packets, 1)]
    (weight_grad,) = local_call(
        weight_grad_kernel, [jax.ShapeDtypeStruct(weight.shape, BF16)], place, tokens, *mine, *other, cots
    )
    keys, input_grad = local_call(
        finish_kernel,
        [jax.ShapeDtypeStruct((rows, cols), BF16), jax.ShapeDtypeStruct((summed.shape[0] // shards, tokens.shape[1]), BF16)],
        place, None, keys_own, summed, *packets,
    )
    return keys, input_grad, weight_grad


def body(tokens, key_weight, key_cotangent, local_frag, outer_frag, momentum):
    weight = key_weight[0]
    islands = lax.axis_size("island")
    if islands != 2:
        cots, part, mine = gather(tokens, weight, key_cotangent)
        state = combine(cots, part, mine, tokens, weight)
        keys, input_grad, weight_grad = finish(cots, mine, *state, tokens, weight)
        frag_sum = lax.psum(local_frag[0], "island").astype(F32)
        new_outer, new_momentum = nesterov(frag_sum, outer_frag, momentum, islands)
        return (keys, input_grad, weight_grad[None], new_outer, new_momentum)

    theirs = [swapped(*pieces_of(local_frag, [0]))]
    cots, part, mine = together(gather, tokens, weight, key_cotangent)

    def step_two(cots, part, mine, tokens, weight, local_frag):
        return combine(cots, part, mine, tokens, weight), pieces_of(local_frag, range(1, len(chunk_units)), hint=6 * 10**9)

    state, pieces = together(step_two, cots, part, mine, tokens, weight, local_frag)
    theirs += [swapped(piece) for piece in pieces]
    theirs[0], state = lax.optimization_barrier((theirs[0], state))

    def step_three(theirs, cots, mine, state, tokens, weight, *frag):
        return finish(cots, mine, *state, tokens, weight), update(0, theirs, *frag, ())

    results, done = together(
        step_three, theirs[0], cots, mine, state, tokens, weight, local_frag, outer_frag, momentum
    )
    keys, input_grad, weight_grad = results
    for k in range(1, len(theirs)):
        theirs[k], done = lax.optimization_barrier((theirs[k], done))
        done = update(k, theirs[k], local_frag, outer_frag, momentum, done)
    new_outer, new_momentum = (a.reshape(outer_frag.shape) for a in done)
    return (keys, input_grad, weight_grad[None], new_outer, new_momentum)


def solution(mesh):
    return jax.shard_map(
        body,
        mesh=mesh,
        in_specs=(
            P(("island", "fsdp"), None),
            P("island", "fsdp", "tensor"),
            P(("island", "fsdp"), "tensor"),
            P("island", None, "fsdp", "tensor"),
            P(None, "fsdp", "tensor"),
            P(None, "fsdp", "tensor"),
        ),
        out_specs=(
            P(("island", "fsdp"), "tensor"),
            P(("island", "fsdp", "tensor"), None),
            P("island", "fsdp", "tensor"),
            P(None, "fsdp", "tensor"),
            P(None, "fsdp", "tensor"),
        ),
        check_vma=False,
    )
```

```python
import functools

import jax
import jax.numpy as jnp
from jax import lax
from jax.experimental import pallas as pl
from jax.experimental.pallas import tpu as pltpu
from jax.sharding import PartitionSpec as P

outer_rate = 0.7
beta_outer = 0.9
F32 = jnp.float32
BF16 = jnp.bfloat16
units = 32
chunk_units = ((0, 19, 4), (19, 10, 2), (29, 3, None))


def nesterov(frag_sum, outer, momentum, islands):
    average = outer - frag_sum / islands
    new_momentum = beta_outer * momentum + average
    return outer - outer_rate * (average + beta_outer * new_momentum), new_momentum


def update_kernel(islands, first, cuts, theirs, ours, outer, momentum, *refs):
    new_outer, new_momentum, their_rows, our_rows, outer_rows, momentum_rows, loads, stores = refs[-8:]
    arriving, leaving = [], []
    for k, (top, bottom) in enumerate(zip(cuts, cuts[1:])):
        here, there = pl.ds(top, bottom - top), pl.ds(first + top, bottom - top)
        sources = (theirs.at[here], ours.at[there], outer.at[there], momentum.at[there])
        buffers = (their_rows, our_rows, outer_rows, momentum_rows)
        arriving.append([pltpu.make_async_copy(s, b.at[here], loads.at[i, k]) for i, (s, b) in enumerate(zip(sources, buffers))])
        results = ((outer_rows, new_outer), (momentum_rows, new_momentum))
        leaving.append([pltpu.make_async_copy(b.at[here], d.at[there], stores.at[i, k]) for i, (b, d) in enumerate(results)])
    for copies in arriving:
        for copy in copies:
            copy.start()
    for (top, bottom), copies, results in zip(zip(cuts, cuts[1:]), arriving, leaving):
        for copy in copies:
            copy.wait()
        rows = slice(top, bottom)
        frag_sum = our_rows[rows].astype(F32) + their_rows[rows].astype(F32)
        outer_rows[rows], momentum_rows[rows] = nesterov(frag_sum, outer_rows[rows], momentum_rows[rows], islands)
        for copy in results:
            copy.start()
    for copies in leaving:
        for copy in copies:
            copy.wait()


def own_terms(k, local_frag, outer_frag, momentum):
    ours, outer, held = (a.reshape(-1, a.shape[-1]) for a in (local_frag, outer_frag, momentum))
    unit = ours.shape[0] // units
    first, size, _ = chunk_units[k]
    ours, outer, held = (lax.slice_in_dim(a, first * unit, (first + size) * unit) for a in (ours, outer, held))
    return nesterov(ours.astype(F32), outer, held, lax.axis_size("island"))


def last_update(theirs, terms, done):
    share = theirs.astype(F32) / lax.axis_size("island")
    results = terms[0] + outer_rate * (1 + beta_outer) * share, terms[1] - share
    first = done[0].shape[0] - theirs.shape[0]
    return [lax.dynamic_update_slice(whole, part, (first, 0)) for whole, part in zip(done, results)]


def update(k, theirs, local_frag, outer_frag, momentum, done):
    islands = lax.axis_size("island")
    ours, outer, held = (a.reshape(-1, a.shape[-1]) for a in (local_frag, outer_frag, momentum))
    unit = ours.shape[0] // units
    (first, size, parts), cols = chunk_units[k], ours.shape[1]
    first, rows = first * unit, size * unit
    cuts = [rows * i // parts // 16 * 16 for i in range(parts)] + [rows]
    hbm = pl.BlockSpec(memory_space=pltpu.HBM)
    return pl.pallas_call(
        functools.partial(update_kernel, islands, first, cuts),
        in_specs=[hbm] * (4 + len(done)),
        out_specs=[hbm] * 2,
        out_shape=[jax.ShapeDtypeStruct(outer.shape, F32)] * 2,
        scratch_shapes=[pltpu.VMEM((rows, cols), BF16)] * 2
        + [pltpu.VMEM((rows, cols), F32)] * 2
        + [pltpu.SemaphoreType.DMA((4, parts)), pltpu.SemaphoreType.DMA((2, parts))],
        input_output_aliases={4 + i: i for i in range(len(done))},
        compiler_params=pltpu.CompilerParams(vmem_limit_bytes=32 * 1024 * 1024),
        cost_estimate=pl.CostEstimate(flops=0, bytes_accessed=0, transcendentals=0),
    )(theirs, ours, outer, held, *done)


def piece_kernel(parts, ours, *refs):
    pieces, loads = refs[:-1], refs[-1]
    copies = []
    for (first, cuts), piece in zip(parts, pieces):
        for top, bottom in zip(cuts, cuts[1:]):
            source = ours.at[pl.ds(first + top, bottom - top)]
            copies.append(pltpu.make_async_copy(source, piece.at[pl.ds(top, bottom - top)], loads.at[len(copies)]))
    for copy in copies:
        copy.start()
    for copy in copies:
        copy.wait()


def pieces_of(local_frag, members, hint=0):
    ours = local_frag.reshape(-1, local_frag.shape[-1])
    unit, cols = ours.shape[0] // units, ours.shape[1]
    shapes = [(chunk_units[k][1] * unit, cols) for k in members]
    parts = []
    for k, (rows, _) in zip(members, shapes):
        cuts = list(range(0, rows, 5 * unit)) + [rows]
        parts.append((chunk_units[k][0] * unit, cuts))
    copies = sum(len(cuts) - 1 for _, cuts in parts)
    return pl.pallas_call(
        functools.partial(piece_kernel, parts),
        in_specs=[pl.BlockSpec(memory_space=pltpu.HBM)],
        out_specs=[pl.BlockSpec(memory_space=pltpu.VMEM)] * len(members),
        out_shape=[pltpu.VMEM(s, BF16) if k == 0 else jax.ShapeDtypeStruct(s, BF16) for k, s in zip(members, shapes)],
        scratch_shapes=[pltpu.SemaphoreType.DMA((copies,))],
        compiler_params=pltpu.CompilerParams(vmem_limit_bytes=16 * 1024 * 1024),
        cost_estimate=pl.CostEstimate(flops=hint, bytes_accessed=0, transcendentals=0),
    )(ours)


def swapped(piece):
    return lax.ppermute(piece, "island", [(0, 1), (1, 0)])


def together(f, *operands):
    shapes = jax.eval_shape(f, *operands)
    return lax.cond(
        lax.axis_index("fsdp") >= 0, f, lambda *_: jax.tree.map(lambda s: jnp.zeros(s.shape, s.dtype), shapes), *operands
    )


def shifted(x, axis, step):
    n = lax.axis_size(axis)
    return lax.ppermute(x, axis, [(i, (i + step) % n) for i in range(n)])


def paired(x, axis, bit):
    return lax.ppermute(x, axis, [(i, i ^ bit) for i in range(lax.axis_size(axis))])


def leaving_at(axis, bit):
    return [lax.axis_index(axis) ^ k for k in range(bit, lax.axis_size(axis), 2 * bit)]


def input_terms(cots, weight):
    share = cots.shape[1] // lax.axis_size("tensor")

    def part_of(members):
        rows_of = jnp.concatenate([lax.dynamic_slice_in_dim(cots, m * share, share, 1) for m in members])
        return lax.dot_general(
            rows_of.reshape(-1, cots.shape[2]), weight, (((1,), (1,)), ((), ())), preferred_element_type=F32
        )

    return part_of


def sum_scatter(came, part_of, axis):
    n = lax.axis_size(axis)
    received = {k: [] for k in range(n)}
    bit = 1
    while bit < n:
        leaving = list(range(bit, n, 2 * bit))
        if bit > 1:
            part = part_of(leaving_at(axis, bit))
            for terms in zip(*(received[k] for k in leaving)):
                part = part + jnp.concatenate([t.astype(F32) for t in terms])
            came = paired(part.astype(BF16), axis, bit)
        for slot, block in zip(leaving, jnp.split(came, len(leaving))):
            received[slot ^ bit].append(block)
        bit *= 2
    return part_of([lax.axis_index(axis)]) + sum(t.astype(F32) for t in received[0])


def keys_kernel(place, own, *refs):
    peers = (len(refs) - 3) // 3
    mine, other = refs[:peers], refs[peers : 2 * peers]
    weight, summed, keys_own, *packets = refs[2 * peers :]
    core = place[1]
    half, cols = own.shape[0] // 2, weight.shape[1]
    share = summed.shape[0] // (peers + 1)
    rows = jnp.concatenate([own[...]] + [block[...] for block in (*mine, *other)])
    part = jnp.dot(rows, weight[...], preferred_element_type=F32)
    keys_own[...] = part[: 2 * half]
    part = part.astype(BF16)
    for s, packet in enumerate(packets):
        for top, at in ((2 + s) * half, core), ((2 + peers + s) * half, 1 - core):
            packet[pl.ds(pl.multiple_of(at * half, half), half), :] = part[top : top + half]
    for s, packet in enumerate(packets, 1):
        for j in range(summed.shape[1] // cols):
            top = 2 * half + j * share
            packet[top : top + share, :] = summed[s * share : (s + 1) * share, j * cols : (j + 1) * cols]


def finish_kernel(place, keys_own, summed, *refs):
    packets, (keys, input_grad) = refs[:-2], refs[-2:]
    shards = len(packets) + 1
    rows, cols = keys.shape
    share, width = input_grad.shape[0], summed.shape[1]
    total = keys_own[...]
    for packet in packets:
        total = total + packet[:rows, :].astype(F32)
    keys[...] = total.astype(BF16)
    input_grad[:, pl.ds(pl.multiple_of(place[0] * width, width), width)] = summed[:share, :]
    for s, packet in enumerate(packets, 1):
        origin = lax.rem(place[0] + s, shards) * width
        for j in range(width // cols):
            top = rows + j * share
            input_grad[:, pl.ds(pl.multiple_of(origin + j * cols, cols), cols)] = packet[top : top + share, :]


def weight_grad_kernel(place, own, *refs):
    peers = (len(refs) - 2) // 2
    mine, other, (cots, weight_grad) = refs[:peers], refs[peers : 2 * peers], refs[2 * peers :]
    core = place[1]
    half = own.shape[0] // 2
    tokens, rows = [own[...]], [cots[0]]
    for blocks, at in ((mine, core), (other, 1 - core)):
        for s, block in enumerate(blocks, 1):
            tokens.append(block[...])
            rows.append(cots[s, pl.ds(pl.multiple_of(at * half, half), half), :])
    total = lax.dot_general(
        jnp.concatenate(tokens), jnp.concatenate(rows), (((0,), (0,)), ((), ())), preferred_element_type=F32
    )
    weight_grad[...] = total.astype(BF16)


def local_call(kernel, out_shape, place, tokens, *operands, flops=0):
    whole = pl.BlockSpec(memory_space=pltpu.VMEM)
    first = [] if tokens is None else [tokens]
    width = first[0].shape[1] // lax.axis_size("fsdp") if first else 0
    columns = [pl.BlockSpec((a.shape[0], width), lambda i, place: (0, place[0])) for a in first]
    return pl.pallas_call(
        kernel,
        grid_spec=pltpu.PrefetchScalarGridSpec(
            num_scalar_prefetch=1, grid=(1,), in_specs=columns + [whole] * len(operands), out_specs=[whole] * len(out_shape)
        ),
        out_shape=out_shape,
        compiler_params=pltpu.CompilerParams(vmem_limit_bytes=32 * 1024 * 1024),
        cost_estimate=pl.CostEstimate(flops=flops, bytes_accessed=0, transcendentals=0),
    )(place, *first, *operands)


def place_of():
    return lax.axis_index("fsdp"), lax.rem(lax.axis_index("tensor"), 2)


def columns_for(tokens, s, width):
    me, core = place_of()
    half = tokens.shape[0] // 2
    return lax.dynamic_slice(tokens, (core * half, lax.rem(me + s, lax.axis_size("fsdp")) * width), (half, width))


def gather(tokens, weight, cotangent):
    cots = jnp.stack([cotangent] + [shifted(cotangent, "fsdp", s) for s in range(1, lax.axis_size("fsdp"))])
    part = input_terms(cots, weight)(leaving_at("tensor", 1)).astype(BF16)
    return cots, part, shifted(columns_for(tokens, 1, weight.shape[0]), "fsdp", 1)


def combine(cots, part, mine, tokens, weight):
    place = jnp.stack(place_of()).astype(jnp.int32)
    shards, heads = lax.axis_size("fsdp"), lax.axis_size("tensor")
    width, cols = weight.shape
    rows = tokens.shape[0]
    share = rows // heads

    part = paired(part, "tensor", 1)
    mine = [mine] + [shifted(columns_for(tokens, s, width), "fsdp", s) for s in range(2, shards)]
    other = [paired(block, "tensor", 1) for block in mine]
    summed = sum_scatter(part, input_terms(cots, weight), "tensor").astype(BF16)
    packet = jax.ShapeDtypeStruct((rows + share * width // cols, cols), BF16)
    keys_own, *packets = local_call(
        keys_kernel,
        [jax.ShapeDtypeStruct((rows, cols), F32)] + [packet] * (shards - 1),
        place, tokens, *mine, *other, weight, summed,
    )
    return mine[1:], other, (keys_own, summed), packets


def finish(cots, mine, more, other, own, packets, tokens, weight):
    place = jnp.stack(place_of()).astype(jnp.int32)
    mine = [mine, *more]
    keys_own, summed = own
    shards, rows, cols = cots.shape
    packets = [shifted(p, "fsdp", -s) for s, p in enumerate(packets, 1)]
    (weight_grad,) = local_call(
        weight_grad_kernel, [jax.ShapeDtypeStruct(weight.shape, BF16)], place, tokens, *mine, *other, cots
    )
    keys, input_grad = local_call(
        finish_kernel,
        [jax.ShapeDtypeStruct((rows, cols), BF16), jax.ShapeDtypeStruct((summed.shape[0] // shards, tokens.shape[1]), BF16)],
        place, None, keys_own, summed, *packets,
    )
    return keys, input_grad, weight_grad


def body(tokens, key_weight, key_cotangent, local_frag, outer_frag, momentum):
    weight = key_weight[0]
    islands = lax.axis_size("island")
    if islands != 2:
        cots, part, mine = gather(tokens, weight, key_cotangent)
        state = combine(cots, part, mine, tokens, weight)
        keys, input_grad, weight_grad = finish(cots, mine, *state, tokens, weight)
        frag_sum = lax.psum(local_frag[0], "island").astype(F32)
        new_outer, new_momentum = nesterov(frag_sum, outer_frag, momentum, islands)
        return (keys, input_grad, weight_grad[None], new_outer, new_momentum)

    theirs = [swapped(*pieces_of(local_frag, [0]))]
    cots, part, mine = together(gather, tokens, weight, key_cotangent)

    def step_two(cots, part, mine, tokens, weight, local_frag):
        return combine(cots, part, mine, tokens, weight), pieces_of(local_frag, range(1, len(chunk_units)), hint=6 * 10**9)

    state, pieces = together(step_two, cots, part, mine, tokens, weight, local_frag)
    theirs.append(swapped(pieces[0]))
    theirs[0], state = lax.optimization_barrier((theirs[0], state))

    def step_three(theirs, cots, mine, state, tokens, weight, *frag):
        return finish(cots, mine, *state, tokens, weight), update(0, theirs, *frag, ()), own_terms(2, *frag)

    results, done, terms = together(
        step_three, theirs[0], cots, mine, state, tokens, weight, local_frag, outer_frag, momentum
    )
    keys, input_grad, weight_grad = results
    piece, done = lax.optimization_barrier((pieces[1], done))
    theirs.append(swapped(piece))
    theirs[1], done = lax.optimization_barrier((theirs[1], done))
    done = update(1, theirs[1], local_frag, outer_frag, momentum, done)
    done = last_update(theirs[2], terms, done)
    new_outer, new_momentum = (a.reshape(outer_frag.shape) for a in done)
    return (keys, input_grad, weight_grad[None], new_outer, new_momentum)


def solution(mesh):
    return jax.shard_map(
        body,
        mesh=mesh,
        in_specs=(
            P(("island", "fsdp"), None),
            P("island", "fsdp", "tensor"),
            P(("island", "fsdp"), "tensor"),
            P("island", None, "fsdp", "tensor"),
            P(None, "fsdp", "tensor"),
            P(None, "fsdp", "tensor"),
        ),
        out_specs=(
            P(("island", "fsdp"), "tensor"),
            P(("island", "fsdp", "tensor"), None),
            P("island", "fsdp", "tensor"),
            P(None, "fsdp", "tensor"),
            P(None, "fsdp", "tensor"),
        ),
        check_vma=False,
    )
```

```python
import functools

import jax
import jax.numpy as jnp
from jax import lax
from jax.experimental import pallas as pl
from jax.experimental.pallas import tpu as pltpu
from jax.sharding import PartitionSpec as P

outer_rate = 0.7
beta_outer = 0.9
F32 = jnp.float32
BF16 = jnp.bfloat16
units = 32
chunk_units = ((0, 19, 6), (19, 10, 3), (29, 3, None))


def nesterov(frag_sum, outer, momentum, islands):
    average = outer - frag_sum / islands
    new_momentum = beta_outer * momentum + average
    return outer - outer_rate * (average + beta_outer * new_momentum), new_momentum


def update_kernel(islands, first, cuts, theirs, ours, outer, momentum, *refs):
    new_outer, new_momentum, their_rows, our_rows, outer_rows, momentum_rows, loads, stores = refs[-8:]
    arriving, leaving = [], []
    for k, (top, bottom) in enumerate(zip(cuts, cuts[1:])):
        here, there = pl.ds(top, bottom - top), pl.ds(first + top, bottom - top)
        sources = (theirs.at[here], ours.at[there], outer.at[there], momentum.at[there])
        buffers = (their_rows, our_rows, outer_rows, momentum_rows)
        arriving.append([pltpu.make_async_copy(s, b.at[here], loads.at[i, k]) for i, (s, b) in enumerate(zip(sources, buffers))])
        results = ((outer_rows, new_outer), (momentum_rows, new_momentum))
        leaving.append([pltpu.make_async_copy(b.at[here], d.at[there], stores.at[i, k]) for i, (b, d) in enumerate(results)])
    for copies in arriving:
        for copy in copies:
            copy.start()
    for (top, bottom), copies, results in zip(zip(cuts, cuts[1:]), arriving, leaving):
        for copy in copies:
            copy.wait()
        rows = slice(top, bottom)
        frag_sum = our_rows[rows].astype(F32) + their_rows[rows].astype(F32)
        outer_rows[rows], momentum_rows[rows] = nesterov(frag_sum, outer_rows[rows], momentum_rows[rows], islands)
        for copy in results:
            copy.start()
    for copies in leaving:
        for copy in copies:
            copy.wait()


def own_terms(k, local_frag, outer_frag, momentum):
    ours, outer, held = (a.reshape(-1, a.shape[-1]) for a in (local_frag, outer_frag, momentum))
    unit = ours.shape[0] // units
    first, size, _ = chunk_units[k]
    ours, outer, held = (lax.slice_in_dim(a, first * unit, (first + size) * unit) for a in (ours, outer, held))
    return nesterov(ours.astype(F32), outer, held, lax.axis_size("island"))


def last_update(theirs, terms, done):
    share = theirs.astype(F32) / lax.axis_size("island")
    results = terms[0] + outer_rate * (1 + beta_outer) * share, terms[1] - share
    first = done[0].shape[0] - theirs.shape[0]
    return [lax.dynamic_update_slice(whole, part, (first, 0)) for whole, part in zip(done, results)]


def update(k, theirs, local_frag, outer_frag, momentum, done):
    islands = lax.axis_size("island")
    ours, outer, held = (a.reshape(-1, a.shape[-1]) for a in (local_frag, outer_frag, momentum))
    unit = ours.shape[0] // units
    (first, size, parts), cols = chunk_units[k], ours.shape[1]
    first, rows = first * unit, size * unit
    cuts = [rows * i // parts // 16 * 16 for i in range(parts)] + [rows]
    hbm = pl.BlockSpec(memory_space=pltpu.HBM)
    return pl.pallas_call(
        functools.partial(update_kernel, islands, first, cuts),
        in_specs=[hbm] * (4 + len(done)),
        out_specs=[hbm] * 2,
        out_shape=[jax.ShapeDtypeStruct(outer.shape, F32)] * 2,
        scratch_shapes=[pltpu.VMEM((rows, cols), BF16)] * 2
        + [pltpu.VMEM((rows, cols), F32)] * 2
        + [pltpu.SemaphoreType.DMA((4, parts)), pltpu.SemaphoreType.DMA((2, parts))],
        input_output_aliases={4 + i: i for i in range(len(done))},
        compiler_params=pltpu.CompilerParams(vmem_limit_bytes=(44 if done else 32) * 1024 * 1024),
        cost_estimate=pl.CostEstimate(flops=0, bytes_accessed=0, transcendentals=0),
    )(theirs, ours, outer, held, *done)


def piece_kernel(parts, ours, *refs):
    pieces, loads = refs[:-1], refs[-1]
    copies = []
    for (first, cuts), piece in zip(parts, pieces):
        for top, bottom in zip(cuts, cuts[1:]):
            source = ours.at[pl.ds(first + top, bottom - top)]
            copies.append(pltpu.make_async_copy(source, piece.at[pl.ds(top, bottom - top)], loads.at[len(copies)]))
    for copy in copies:
        copy.start()
    for copy in copies:
        copy.wait()


def pieces_of(local_frag, members, hint=0):
    ours = local_frag.reshape(-1, local_frag.shape[-1])
    unit, cols = ours.shape[0] // units, ours.shape[1]
    shapes = [(chunk_units[k][1] * unit, cols) for k in members]
    parts = []
    for k, (rows, _) in zip(members, shapes):
        cuts = list(range(0, rows, 10 * unit)) + [rows]
        parts.append((chunk_units[k][0] * unit, cuts))
    copies = sum(len(cuts) - 1 for _, cuts in parts)
    return pl.pallas_call(
        functools.partial(piece_kernel, parts),
        in_specs=[pl.BlockSpec(memory_space=pltpu.HBM)],
        out_specs=[pl.BlockSpec(memory_space=pltpu.VMEM)] * len(members),
        out_shape=[pltpu.VMEM(s, BF16) if k == 0 else jax.ShapeDtypeStruct(s, BF16) for k, s in zip(members, shapes)],
        scratch_shapes=[pltpu.SemaphoreType.DMA((copies,))],
        compiler_params=pltpu.CompilerParams(vmem_limit_bytes=8 * 1024 * 1024),
        cost_estimate=pl.CostEstimate(flops=hint, bytes_accessed=0, transcendentals=0),
    )(ours)


def swapped(piece):
    return lax.ppermute(piece, "island", [(0, 1), (1, 0)])


def together(f, *operands):
    shapes = jax.eval_shape(f, *operands)
    return lax.cond(
        lax.axis_index("fsdp") >= 0, f, lambda *_: jax.tree.map(lambda s: jnp.zeros(s.shape, s.dtype), shapes), *operands
    )


def shifted(x, axis, step):
    n = lax.axis_size(axis)
    return lax.ppermute(x, axis, [(i, (i + step) % n) for i in range(n)])


def paired(x, axis, bit):
    return lax.ppermute(x, axis, [(i, i ^ bit) for i in range(lax.axis_size(axis))])


def leaving_at(axis, bit):
    return [lax.axis_index(axis) ^ k for k in range(bit, lax.axis_size(axis), 2 * bit)]


def input_terms(cots, weight):
    share = cots.shape[1] // lax.axis_size("tensor")

    def part_of(members):
        rows_of = jnp.concatenate([lax.dynamic_slice_in_dim(cots, m * share, share, 1) for m in members])
        return lax.dot_general(
            rows_of.reshape(-1, cots.shape[2]), weight, (((1,), (1,)), ((), ())), preferred_element_type=F32
        )

    return part_of


def sum_scatter(came, part_of, axis):
    n = lax.axis_size(axis)
    received = {k: [] for k in range(n)}
    bit = 1
    while bit < n:
        leaving = list(range(bit, n, 2 * bit))
        if bit > 1:
            part = part_of(leaving_at(axis, bit))
            for terms in zip(*(received[k] for k in leaving)):
                part = part + jnp.concatenate([t.astype(F32) for t in terms])
            came = paired(part.astype(BF16), axis, bit)
        for slot, block in zip(leaving, jnp.split(came, len(leaving))):
            received[slot ^ bit].append(block)
        bit *= 2
    return part_of([lax.axis_index(axis)]) + sum(t.astype(F32) for t in received[0])


def keys_kernel(place, own, *refs):
    peers = (len(refs) - 3) // 3
    mine, other = refs[:peers], refs[peers : 2 * peers]
    weight, summed, keys_own, *packets = refs[2 * peers :]
    core = place[1]
    half, cols = own.shape[0] // 2, weight.shape[1]
    share = summed.shape[0] // (peers + 1)
    rows = jnp.concatenate([own[...]] + [block[...] for block in (*mine, *other)])
    part = jnp.dot(rows, weight[...], preferred_element_type=F32)
    keys_own[...] = part[: 2 * half]
    part = part.astype(BF16)
    for s, packet in enumerate(packets):
        for top, at in ((2 + s) * half, core), ((2 + peers + s) * half, 1 - core):
            packet[pl.ds(pl.multiple_of(at * half, half), half), :] = part[top : top + half]
    for s, packet in enumerate(packets, 1):
        for j in range(summed.shape[1] // cols):
            top = 2 * half + j * share
            packet[top : top + share, :] = summed[s * share : (s + 1) * share, j * cols : (j + 1) * cols]


def finish_kernel(place, keys_own, summed, *refs):
    packets, (keys, input_grad) = refs[:-2], refs[-2:]
    shards = len(packets) + 1
    rows, cols = keys.shape
    share, width = input_grad.shape[0], summed.shape[1]
    total = keys_own[...]
    for packet in packets:
        total = total + packet[:rows, :].astype(F32)
    keys[...] = total.astype(BF16)
    input_grad[:, pl.ds(pl.multiple_of(place[0] * width, width), width)] = summed[:share, :]
    for s, packet in enumerate(packets, 1):
        origin = lax.rem(place[0] + s, shards) * width
        for j in range(width // cols):
            top = rows + j * share
            input_grad[:, pl.ds(pl.multiple_of(origin + j * cols, cols), cols)] = packet[top : top + share, :]


def weight_grad_kernel(place, own, *refs):
    peers = (len(refs) - 2) // 2
    mine, other, (cots, weight_grad) = refs[:peers], refs[peers : 2 * peers], refs[2 * peers :]
    core = place[1]
    half = own.shape[0] // 2
    tokens, rows = [own[...]], [cots[0]]
    for blocks, at in ((mine, core), (other, 1 - core)):
        for s, block in enumerate(blocks, 1):
            tokens.append(block[...])
            rows.append(cots[s, pl.ds(pl.multiple_of(at * half, half), half), :])
    total = lax.dot_general(
        jnp.concatenate(tokens), jnp.concatenate(rows), (((0,), (0,)), ((), ())), preferred_element_type=F32
    )
    weight_grad[...] = total.astype(BF16)


def local_call(kernel, out_shape, place, tokens, *operands, flops=0):
    whole = pl.BlockSpec(memory_space=pltpu.VMEM)
    first = [] if tokens is None else [tokens]
    width = first[0].shape[1] // lax.axis_size("fsdp") if first else 0
    columns = [pl.BlockSpec((a.shape[0], width), lambda i, place: (0, place[0])) for a in first]
    return pl.pallas_call(
        kernel,
        grid_spec=pltpu.PrefetchScalarGridSpec(
            num_scalar_prefetch=1, grid=(1,), in_specs=columns + [whole] * len(operands), out_specs=[whole] * len(out_shape)
        ),
        out_shape=out_shape,
        compiler_params=pltpu.CompilerParams(vmem_limit_bytes=12 * 1024 * 1024),
        cost_estimate=pl.CostEstimate(flops=flops, bytes_accessed=0, transcendentals=0),
    )(place, *first, *operands)


def place_of():
    return lax.axis_index("fsdp"), lax.rem(lax.axis_index("tensor"), 2)


def columns_for(tokens, s, width):
    me, core = place_of()
    half = tokens.shape[0] // 2
    return lax.dynamic_slice(tokens, (core * half, lax.rem(me + s, lax.axis_size("fsdp")) * width), (half, width))


def gather(tokens, weight, cotangent):
    cots = jnp.stack([cotangent] + [shifted(cotangent, "fsdp", s) for s in range(1, lax.axis_size("fsdp"))])
    part = input_terms(cots, weight)(leaving_at("tensor", 1)).astype(BF16)
    return cots, part, shifted(columns_for(tokens, 1, weight.shape[0]), "fsdp", 1)


def combine(cots, part, mine, tokens, weight):
    place = jnp.stack(place_of()).astype(jnp.int32)
    shards, heads = lax.axis_size("fsdp"), lax.axis_size("tensor")
    width, cols = weight.shape
    rows = tokens.shape[0]
    share = rows // heads

    part = paired(part, "tensor", 1)
    mine = [mine] + [shifted(columns_for(tokens, s, width), "fsdp", s) for s in range(2, shards)]
    other = [paired(block, "tensor", 1) for block in mine]
    summed = sum_scatter(part, input_terms(cots, weight), "tensor").astype(BF16)
    packet = jax.ShapeDtypeStruct((rows + share * width // cols, cols), BF16)
    keys_own, *packets = local_call(
        keys_kernel,
        [jax.ShapeDtypeStruct((rows, cols), F32)] + [packet] * (shards - 1),
        place, tokens, *mine, *other, weight, summed,
    )
    return mine[1:], other, (keys_own, summed), packets


def finish(cots, mine, more, other, own, packets, tokens, weight):
    place = jnp.stack(place_of()).astype(jnp.int32)
    mine = [mine, *more]
    keys_own, summed = own
    shards, rows, cols = cots.shape
    packets = [shifted(p, "fsdp", -s) for s, p in enumerate(packets, 1)]
    (weight_grad,) = local_call(
        weight_grad_kernel, [jax.ShapeDtypeStruct(weight.shape, BF16)], place, tokens, *mine, *other, cots
    )
    keys, input_grad = local_call(
        finish_kernel,
        [jax.ShapeDtypeStruct((rows, cols), BF16), jax.ShapeDtypeStruct((summed.shape[0] // shards, tokens.shape[1]), BF16)],
        place, None, keys_own, summed, *packets,
    )
    return keys, input_grad, weight_grad


def body(tokens, key_weight, key_cotangent, local_frag, outer_frag, momentum):
    weight = key_weight[0]
    islands = lax.axis_size("island")
    if islands != 2:
        cots, part, mine = gather(tokens, weight, key_cotangent)
        state = combine(cots, part, mine, tokens, weight)
        keys, input_grad, weight_grad = finish(cots, mine, *state, tokens, weight)
        frag_sum = lax.psum(local_frag[0], "island").astype(F32)
        new_outer, new_momentum = nesterov(frag_sum, outer_frag, momentum, islands)
        return (keys, input_grad, weight_grad[None], new_outer, new_momentum)

    theirs = [swapped(*pieces_of(local_frag, [0]))]
    cots, part, mine = together(gather, tokens, weight, key_cotangent)

    def step_two(cots, part, mine, tokens, weight, local_frag):
        return combine(cots, part, mine, tokens, weight), pieces_of(local_frag, range(1, len(chunk_units)), hint=6 * 10**9)

    state, pieces = together(step_two, cots, part, mine, tokens, weight, local_frag)
    theirs.append(swapped(pieces[0]))
    theirs[0], state = lax.optimization_barrier((theirs[0], state))

    def step_three(theirs, cots, mine, state, tokens, weight, *frag):
        return finish(cots, mine, *state, tokens, weight), update(0, theirs, *frag, ()), own_terms(2, *frag)

    results, done, terms = together(
        step_three, theirs[0], cots, mine, state, tokens, weight, local_frag, outer_frag, momentum
    )
    keys, input_grad, weight_grad = results
    piece, done = lax.optimization_barrier((pieces[1], done))
    theirs.append(swapped(piece))
    theirs[1], done = lax.optimization_barrier((theirs[1], done))
    done = update(1, theirs[1], local_frag, outer_frag, momentum, done)
    done = last_update(theirs[2], terms, done)
    new_outer, new_momentum = (a.reshape(outer_frag.shape) for a in done)
    return (keys, input_grad, weight_grad[None], new_outer, new_momentum)


def solution(mesh):
    return jax.shard_map(
        body,
        mesh=mesh,
        in_specs=(
            P(("island", "fsdp"), None),
            P("island", "fsdp", "tensor"),
            P(("island", "fsdp"), "tensor"),
            P("island", None, "fsdp", "tensor"),
            P(None, "fsdp", "tensor"),
            P(None, "fsdp", "tensor"),
        ),
        out_specs=(
            P(("island", "fsdp"), "tensor"),
            P(("island", "fsdp", "tensor"), None),
            P("island", "fsdp", "tensor"),
            P(None, "fsdp", "tensor"),
            P(None, "fsdp", "tensor"),
        ),
        check_vma=False,
    )
```

```python
import functools

import jax
import jax.numpy as jnp
from jax import lax
from jax.experimental import pallas as pl
from jax.experimental.pallas import tpu as pltpu
from jax.sharding import PartitionSpec as P

outer_rate = 0.7
beta_outer = 0.9
F32 = jnp.float32
BF16 = jnp.bfloat16
units = 32
late_parts = 2
chunk_units = ((0, 19, 6), (19, 9, 3), (28, 2, None), (30, 2, None))


def nesterov(frag_sum, outer, momentum, islands):
    average = outer - frag_sum / islands
    new_momentum = beta_outer * momentum + average
    return outer - outer_rate * (average + beta_outer * new_momentum), new_momentum


def update_kernel(islands, first, cuts, theirs, ours, outer, momentum, *refs):
    new_outer, new_momentum, their_rows, our_rows, outer_rows, momentum_rows, loads, stores = refs[-8:]
    arriving, leaving = [], []
    for k, (top, bottom) in enumerate(zip(cuts, cuts[1:])):
        here, there = pl.ds(top, bottom - top), pl.ds(first + top, bottom - top)
        sources = (theirs.at[here], ours.at[there], outer.at[there], momentum.at[there])
        buffers = (their_rows, our_rows, outer_rows, momentum_rows)
        arriving.append([pltpu.make_async_copy(s, b.at[here], loads.at[i, k]) for i, (s, b) in enumerate(zip(sources, buffers))])
        results = ((outer_rows, new_outer), (momentum_rows, new_momentum))
        leaving.append([pltpu.make_async_copy(b.at[here], d.at[there], stores.at[i, k]) for i, (b, d) in enumerate(results)])
    for copies in arriving:
        for copy in copies:
            copy.start()
    for (top, bottom), copies, results in zip(zip(cuts, cuts[1:]), arriving, leaving):
        for copy in copies:
            copy.wait()
        rows = slice(top, bottom)
        frag_sum = our_rows[rows].astype(F32) + their_rows[rows].astype(F32)
        outer_rows[rows], momentum_rows[rows] = nesterov(frag_sum, outer_rows[rows], momentum_rows[rows], islands)
        for copy in results:
            copy.start()
    for copies in leaving:
        for copy in copies:
            copy.wait()


def own_terms(k, local_frag, outer_frag, momentum):
    ours, outer, held = (a.reshape(-1, a.shape[-1]) for a in (local_frag, outer_frag, momentum))
    unit = ours.shape[0] // units
    first, size, _ = chunk_units[k]
    ours, outer, held = (lax.slice_in_dim(a, first * unit, (first + size) * unit) for a in (ours, outer, held))
    return nesterov(ours.astype(F32), outer, held, lax.axis_size("island"))


def late_kernel(islands, first, cuts, theirs, outer_terms, momentum_terms, *refs):
    new_outer, new_momentum, outer_rows, momentum_rows, stores = refs[-5:]
    leaving = []
    for k, (top, bottom) in enumerate(zip(cuts, cuts[1:])):
        rows, there = slice(top, bottom), pl.ds(first + top, bottom - top)
        share = theirs[rows].astype(F32) / islands
        outer_rows[rows] = outer_terms[rows] + outer_rate * (1 + beta_outer) * share
        momentum_rows[rows] = momentum_terms[rows] - share
        for i, (buffer, out) in enumerate(((outer_rows, new_outer), (momentum_rows, new_momentum))):
            leaving.append(pltpu.make_async_copy(buffer.at[pl.ds(top, bottom - top)], out.at[there], stores.at[i, k]))
            leaving[-1].start()
    for copy in leaving:
        copy.wait()


def late_update(k, theirs, terms, done):
    rows, cols = theirs.shape
    first = chunk_units[k][0] * (done[0].shape[0] // units)
    cuts = [rows * i // late_parts // 16 * 16 for i in range(late_parts)] + [rows]
    hbm, vmem = pl.BlockSpec(memory_space=pltpu.HBM), pl.BlockSpec(memory_space=pltpu.VMEM)
    return pl.pallas_call(
        functools.partial(late_kernel, lax.axis_size("island"), first, cuts),
        in_specs=[vmem] * 3 + [hbm] * 2,
        out_specs=[hbm] * 2,
        out_shape=[jax.ShapeDtypeStruct(a.shape, F32) for a in done],
        scratch_shapes=[pltpu.VMEM((rows, cols), F32)] * 2 + [pltpu.SemaphoreType.DMA((2, late_parts))],
        input_output_aliases={3: 0, 4: 1},
        compiler_params=pltpu.CompilerParams(vmem_limit_bytes=44 * 1024 * 1024),
        cost_estimate=pl.CostEstimate(flops=0, bytes_accessed=0, transcendentals=0),
    )(theirs, *terms, *done)


def update(k, theirs, local_frag, outer_frag, momentum, done):
    islands = lax.axis_size("island")
    ours, outer, held = (a.reshape(-1, a.shape[-1]) for a in (local_frag, outer_frag, momentum))
    unit = ours.shape[0] // units
    (first, size, parts), cols = chunk_units[k], ours.shape[1]
    first, rows = first * unit, size * unit
    cuts = [rows * i // parts // 16 * 16 for i in range(parts)] + [rows]
    hbm = pl.BlockSpec(memory_space=pltpu.HBM)
    return pl.pallas_call(
        functools.partial(update_kernel, islands, first, cuts),
        in_specs=[hbm] * (4 + len(done)),
        out_specs=[hbm] * 2,
        out_shape=[jax.ShapeDtypeStruct(outer.shape, F32)] * 2,
        scratch_shapes=[pltpu.VMEM((rows, cols), BF16)] * 2
        + [pltpu.VMEM((rows, cols), F32)] * 2
        + [pltpu.SemaphoreType.DMA((4, parts)), pltpu.SemaphoreType.DMA((2, parts))],
        input_output_aliases={4 + i: i for i in range(len(done))},
        compiler_params=pltpu.CompilerParams(vmem_limit_bytes=(44 if done else 32) * 1024 * 1024),
        cost_estimate=pl.CostEstimate(flops=0, bytes_accessed=0, transcendentals=0),
    )(theirs, ours, outer, held, *done)


def piece_kernel(parts, ours, *refs):
    pieces, loads = refs[:-1], refs[-1]
    copies = []
    for (first, cuts), piece in zip(parts, pieces):
        for top, bottom in zip(cuts, cuts[1:]):
            source = ours.at[pl.ds(first + top, bottom - top)]
            copies.append(pltpu.make_async_copy(source, piece.at[pl.ds(top, bottom - top)], loads.at[len(copies)]))
    for copy in copies:
        copy.start()
    for copy in copies:
        copy.wait()


def pieces_of(local_frag, members, hint=0):
    ours = local_frag.reshape(-1, local_frag.shape[-1])
    unit, cols = ours.shape[0] // units, ours.shape[1]
    shapes = [(chunk_units[k][1] * unit, cols) for k in members]
    parts = []
    for k, (rows, _) in zip(members, shapes):
        cuts = list(range(0, rows, 10 * unit)) + [rows]
        parts.append((chunk_units[k][0] * unit, cuts))
    copies = sum(len(cuts) - 1 for _, cuts in parts)
    return pl.pallas_call(
        functools.partial(piece_kernel, parts),
        in_specs=[pl.BlockSpec(memory_space=pltpu.HBM)],
        out_specs=[pl.BlockSpec(memory_space=pltpu.VMEM)] * len(members),
        out_shape=[pltpu.VMEM(s, BF16) if k == 0 else jax.ShapeDtypeStruct(s, BF16) for k, s in zip(members, shapes)],
        scratch_shapes=[pltpu.SemaphoreType.DMA((copies,))],
        compiler_params=pltpu.CompilerParams(vmem_limit_bytes=8 * 1024 * 1024),
        cost_estimate=pl.CostEstimate(flops=hint, bytes_accessed=0, transcendentals=0),
    )(ours)


def swapped(piece):
    return lax.ppermute(piece, "island", [(0, 1), (1, 0)])


def together(f, *operands):
    shapes = jax.eval_shape(f, *operands)
    return lax.cond(
        lax.axis_index("fsdp") >= 0, f, lambda *_: jax.tree.map(lambda s: jnp.zeros(s.shape, s.dtype), shapes), *operands
    )


def shifted(x, axis, step):
    n = lax.axis_size(axis)
    return lax.ppermute(x, axis, [(i, (i + step) % n) for i in range(n)])


def paired(x, axis, bit):
    return lax.ppermute(x, axis, [(i, i ^ bit) for i in range(lax.axis_size(axis))])


def leaving_at(axis, bit):
    return [lax.axis_index(axis) ^ k for k in range(bit, lax.axis_size(axis), 2 * bit)]


def input_terms(cots, weight):
    share = cots.shape[1] // lax.axis_size("tensor")

    def part_of(members):
        rows_of = jnp.concatenate([lax.dynamic_slice_in_dim(cots, m * share, share, 1) for m in members])
        return lax.dot_general(
            rows_of.reshape(-1, cots.shape[2]), weight, (((1,), (1,)), ((), ())), preferred_element_type=F32
        )

    return part_of


def sum_scatter(came, part_of, axis):
    n = lax.axis_size(axis)
    received = {k: [] for k in range(n)}
    bit = 1
    while bit < n:
        leaving = list(range(bit, n, 2 * bit))
        if bit > 1:
            part = part_of(leaving_at(axis, bit))
            for terms in zip(*(received[k] for k in leaving)):
                part = part + jnp.concatenate([t.astype(F32) for t in terms])
            came = paired(part.astype(BF16), axis, bit)
        for slot, block in zip(leaving, jnp.split(came, len(leaving))):
            received[slot ^ bit].append(block)
        bit *= 2
    return part_of([lax.axis_index(axis)]) + sum(t.astype(F32) for t in received[0])


def keys_kernel(place, own, *refs):
    peers = (len(refs) - 3) // 3
    mine, other = refs[:peers], refs[peers : 2 * peers]
    weight, summed, keys_own, *packets = refs[2 * peers :]
    core = place[1]
    half, cols = own.shape[0] // 2, weight.shape[1]
    share = summed.shape[0] // (peers + 1)
    rows = jnp.concatenate([own[...]] + [block[...] for block in (*mine, *other)])
    part = jnp.dot(rows, weight[...], preferred_element_type=F32)
    keys_own[...] = part[: 2 * half]
    part = part.astype(BF16)
    for s, packet in enumerate(packets):
        for top, at in ((2 + s) * half, core), ((2 + peers + s) * half, 1 - core):
            packet[pl.ds(pl.multiple_of(at * half, half), half), :] = part[top : top + half]
    for s, packet in enumerate(packets, 1):
        for j in range(summed.shape[1] // cols):
            top = 2 * half + j * share
            packet[top : top + share, :] = summed[s * share : (s + 1) * share, j * cols : (j + 1) * cols]


def finish_kernel(place, keys_own, summed, *refs):
    packets, (keys, input_grad) = refs[:-2], refs[-2:]
    shards = len(packets) + 1
    rows, cols = keys.shape
    share, width = input_grad.shape[0], summed.shape[1]
    total = keys_own[...]
    for packet in packets:
        total = total + packet[:rows, :].astype(F32)
    keys[...] = total.astype(BF16)
    input_grad[:, pl.ds(pl.multiple_of(place[0] * width, width), width)] = summed[:share, :]
    for s, packet in enumerate(packets, 1):
        origin = lax.rem(place[0] + s, shards) * width
        for j in range(width // cols):
            top = rows + j * share
            input_grad[:, pl.ds(pl.multiple_of(origin + j * cols, cols), cols)] = packet[top : top + share, :]


def weight_grad_kernel(place, own, *refs):
    peers = (len(refs) - 2) // 2
    mine, other, (cots, weight_grad) = refs[:peers], refs[peers : 2 * peers], refs[2 * peers :]
    core = place[1]
    half = own.shape[0] // 2
    tokens, rows = [own[...]], [cots[0]]
    for blocks, at in ((mine, core), (other, 1 - core)):
        for s, block in enumerate(blocks, 1):
            tokens.append(block[...])
            rows.append(cots[s, pl.ds(pl.multiple_of(at * half, half), half), :])
    total = lax.dot_general(
        jnp.concatenate(tokens), jnp.concatenate(rows), (((0,), (0,)), ((), ())), preferred_element_type=F32
    )
    weight_grad[...] = total.astype(BF16)


def local_call(kernel, out_shape, place, tokens, *operands, flops=0):
    whole = pl.BlockSpec(memory_space=pltpu.VMEM)
    first = [] if tokens is None else [tokens]
    width = first[0].shape[1] // lax.axis_size("fsdp") if first else 0
    columns = [pl.BlockSpec((a.shape[0], width), lambda i, place: (0, place[0])) for a in first]
    return pl.pallas_call(
        kernel,
        grid_spec=pltpu.PrefetchScalarGridSpec(
            num_scalar_prefetch=1, grid=(1,), in_specs=columns + [whole] * len(operands), out_specs=[whole] * len(out_shape)
        ),
        out_shape=out_shape,
        compiler_params=pltpu.CompilerParams(vmem_limit_bytes=12 * 1024 * 1024),
        cost_estimate=pl.CostEstimate(flops=flops, bytes_accessed=0, transcendentals=0),
    )(place, *first, *operands)


def place_of():
    return lax.axis_index("fsdp"), lax.rem(lax.axis_index("tensor"), 2)


def columns_for(tokens, s, width):
    me, core = place_of()
    half = tokens.shape[0] // 2
    return lax.dynamic_slice(tokens, (core * half, lax.rem(me + s, lax.axis_size("fsdp")) * width), (half, width))


def gather(tokens, weight, cotangent):
    cots = jnp.stack([cotangent] + [shifted(cotangent, "fsdp", s) for s in range(1, lax.axis_size("fsdp"))])
    part = input_terms(cots, weight)(leaving_at("tensor", 1)).astype(BF16)
    return cots, part, shifted(columns_for(tokens, 1, weight.shape[0]), "fsdp", 1)


def combine(cots, part, mine, tokens, weight):
    place = jnp.stack(place_of()).astype(jnp.int32)
    shards, heads = lax.axis_size("fsdp"), lax.axis_size("tensor")
    width, cols = weight.shape
    rows = tokens.shape[0]
    share = rows // heads

    part = paired(part, "tensor", 1)
    mine = [mine] + [shifted(columns_for(tokens, s, width), "fsdp", s) for s in range(2, shards)]
    other = [paired(block, "tensor", 1) for block in mine]
    summed = sum_scatter(part, input_terms(cots, weight), "tensor").astype(BF16)
    packet = jax.ShapeDtypeStruct((rows + share * width // cols, cols), BF16)
    keys_own, *packets = local_call(
        keys_kernel,
        [jax.ShapeDtypeStruct((rows, cols), F32)] + [packet] * (shards - 1),
        place, tokens, *mine, *other, weight, summed,
    )
    return mine[1:], other, (keys_own, summed), packets


def finish(cots, mine, more, other, own, packets, tokens, weight):
    place = jnp.stack(place_of()).astype(jnp.int32)
    mine = [mine, *more]
    keys_own, summed = own
    shards, rows, cols = cots.shape
    packets = [shifted(p, "fsdp", -s) for s, p in enumerate(packets, 1)]
    (weight_grad,) = local_call(
        weight_grad_kernel, [jax.ShapeDtypeStruct(weight.shape, BF16)], place, tokens, *mine, *other, cots
    )
    keys, input_grad = local_call(
        finish_kernel,
        [jax.ShapeDtypeStruct((rows, cols), BF16), jax.ShapeDtypeStruct((summed.shape[0] // shards, tokens.shape[1]), BF16)],
        place, None, keys_own, summed, *packets,
    )
    return keys, input_grad, weight_grad


def body(tokens, key_weight, key_cotangent, local_frag, outer_frag, momentum):
    weight = key_weight[0]
    islands = lax.axis_size("island")
    if islands != 2:
        cots, part, mine = gather(tokens, weight, key_cotangent)
        state = combine(cots, part, mine, tokens, weight)
        keys, input_grad, weight_grad = finish(cots, mine, *state, tokens, weight)
        frag_sum = lax.psum(local_frag[0], "island").astype(F32)
        new_outer, new_momentum = nesterov(frag_sum, outer_frag, momentum, islands)
        return (keys, input_grad, weight_grad[None], new_outer, new_momentum)

    theirs = [swapped(*pieces_of(local_frag, [0]))]
    cots, part, mine = together(gather, tokens, weight, key_cotangent)

    late = range(2, len(chunk_units))

    def step_two(cots, part, mine, tokens, weight, local_frag):
        return combine(cots, part, mine, tokens, weight), pieces_of(local_frag, range(1, len(chunk_units)), hint=6 * 10**9)

    state, pieces = together(step_two, cots, part, mine, tokens, weight, local_frag)
    theirs += [swapped(piece) for piece in pieces[:-1]]
    theirs[0], state = lax.optimization_barrier((theirs[0], state))

    def step_three(theirs, cots, mine, state, tokens, weight, *frag):
        return finish(cots, mine, *state, tokens, weight), update(0, theirs, *frag, ()), [own_terms(k, *frag) for k in late]

    results, done, terms = together(
        step_three, theirs[0], cots, mine, state, tokens, weight, local_frag, outer_frag, momentum
    )
    keys, input_grad, weight_grad = results
    piece, done = lax.optimization_barrier((pieces[-1], done))
    theirs.append(swapped(piece))
    theirs[1], done = lax.optimization_barrier((theirs[1], done))
    done = update(1, theirs[1], local_frag, outer_frag, momentum, done)
    for k in late:
        theirs[k], done = lax.optimization_barrier((theirs[k], done))
        done = late_update(k, theirs[k], terms[k - late[0]], done)
    new_outer, new_momentum = (a.reshape(outer_frag.shape) for a in done)
    return (keys, input_grad, weight_grad[None], new_outer, new_momentum)


def solution(mesh):
    return jax.shard_map(
        body,
        mesh=mesh,
        in_specs=(
            P(("island", "fsdp"), None),
            P("island", "fsdp", "tensor"),
            P(("island", "fsdp"), "tensor"),
            P("island", None, "fsdp", "tensor"),
            P(None, "fsdp", "tensor"),
            P(None, "fsdp", "tensor"),
        ),
        out_specs=(
            P(("island", "fsdp"), "tensor"),
            P(("island", "fsdp", "tensor"), None),
            P("island", "fsdp", "tensor"),
            P(None, "fsdp", "tensor"),
            P(None, "fsdp", "tensor"),
        ),
        check_vma=False,
    )
```

```python
import functools

import jax
import jax.numpy as jnp
from jax import lax
from jax.experimental import pallas as pl
from jax.experimental.pallas import tpu as pltpu
from jax.sharding import PartitionSpec as P

outer_rate = 0.7
beta_outer = 0.9
F32 = jnp.float32
BF16 = jnp.bfloat16
units = 32
late_parts = 2
chunk_units = ((0, 19, 6), (19, 9, 3), (28, 3, None), (31, 1, None))


def nesterov(frag_sum, outer, momentum, islands):
    average = outer - frag_sum / islands
    new_momentum = beta_outer * momentum + average
    return outer - outer_rate * (average + beta_outer * new_momentum), new_momentum


def update_kernel(islands, first, cuts, theirs, ours, outer, momentum, *refs):
    new_outer, new_momentum, their_rows, our_rows, outer_rows, momentum_rows, loads, stores = refs[-8:]
    arriving, leaving = [], []
    for k, (top, bottom) in enumerate(zip(cuts, cuts[1:])):
        here, there = pl.ds(top, bottom - top), pl.ds(first + top, bottom - top)
        sources = (theirs.at[here], ours.at[there], outer.at[there], momentum.at[there])
        buffers = (their_rows, our_rows, outer_rows, momentum_rows)
        arriving.append([pltpu.make_async_copy(s, b.at[here], loads.at[i, k]) for i, (s, b) in enumerate(zip(sources, buffers))])
        results = ((outer_rows, new_outer), (momentum_rows, new_momentum))
        leaving.append([pltpu.make_async_copy(b.at[here], d.at[there], stores.at[i, k]) for i, (b, d) in enumerate(results)])
    for copies in arriving:
        for copy in copies:
            copy.start()
    for (top, bottom), copies, results in zip(zip(cuts, cuts[1:]), arriving, leaving):
        for copy in copies:
            copy.wait()
        rows = slice(top, bottom)
        frag_sum = our_rows[rows].astype(F32) + their_rows[rows].astype(F32)
        outer_rows[rows], momentum_rows[rows] = nesterov(frag_sum, outer_rows[rows], momentum_rows[rows], islands)
        for copy in results:
            copy.start()
    for copies in leaving:
        for copy in copies:
            copy.wait()


def own_terms(late, local_frag, outer_frag, momentum):
    ours, outer, held = (a.reshape(-1, a.shape[-1]) for a in (local_frag, outer_frag, momentum))
    unit = ours.shape[0] // units
    first = chunk_units[late[0]][0]
    last = first + sum(chunk_units[k][1] for k in late)
    ours, outer, held = (lax.slice_in_dim(a, first * unit, last * unit) for a in (ours, outer, held))
    return nesterov(ours.astype(F32), outer, held, lax.axis_size("island"))


def late_kernel(islands, first, skipped, cuts, theirs, outer_terms, momentum_terms, *refs):
    new_outer, new_momentum, outer_rows, momentum_rows, stores = refs[-5:]
    leaving = []
    for k, (top, bottom) in enumerate(zip(cuts, cuts[1:])):
        rows, there = slice(top, bottom), pl.ds(first + top, bottom - top)
        own = slice(skipped + top, skipped + bottom)
        share = theirs[rows].astype(F32) / islands
        outer_rows[rows] = outer_terms[own] + outer_rate * (1 + beta_outer) * share
        momentum_rows[rows] = momentum_terms[own] - share
        for i, (buffer, out) in enumerate(((outer_rows, new_outer), (momentum_rows, new_momentum))):
            leaving.append(pltpu.make_async_copy(buffer.at[pl.ds(top, bottom - top)], out.at[there], stores.at[i, k]))
            leaving[-1].start()
    for copy in leaving:
        copy.wait()


def late_update(k, theirs, terms, done):
    rows, cols = theirs.shape
    first = chunk_units[k][0] * (done[0].shape[0] // units)
    cuts = [rows * i // late_parts // 16 * 16 for i in range(late_parts)] + [rows]
    hbm, vmem = pl.BlockSpec(memory_space=pltpu.HBM), pl.BlockSpec(memory_space=pltpu.VMEM)
    return pl.pallas_call(
        functools.partial(late_kernel, lax.axis_size("island"), first, first - done[0].shape[0] + terms[0].shape[0], cuts),
        in_specs=[vmem] * 3 + [hbm] * 2,
        out_specs=[hbm] * 2,
        out_shape=[jax.ShapeDtypeStruct(a.shape, F32) for a in done],
        scratch_shapes=[pltpu.VMEM((rows, cols), F32)] * 2 + [pltpu.SemaphoreType.DMA((2, late_parts))],
        input_output_aliases={3: 0, 4: 1},
        compiler_params=pltpu.CompilerParams(vmem_limit_bytes=44 * 1024 * 1024),
        cost_estimate=pl.CostEstimate(flops=0, bytes_accessed=0, transcendentals=0),
    )(theirs, *terms, *done)


def update(k, theirs, local_frag, outer_frag, momentum, done):
    islands = lax.axis_size("island")
    ours, outer, held = (a.reshape(-1, a.shape[-1]) for a in (local_frag, outer_frag, momentum))
    unit = ours.shape[0] // units
    (first, size, parts), cols = chunk_units[k], ours.shape[1]
    first, rows = first * unit, size * unit
    cuts = [rows * i // parts // 16 * 16 for i in range(parts)] + [rows]
    hbm = pl.BlockSpec(memory_space=pltpu.HBM)
    return pl.pallas_call(
        functools.partial(update_kernel, islands, first, cuts),
        in_specs=[hbm] * (4 + len(done)),
        out_specs=[hbm] * 2,
        out_shape=[jax.ShapeDtypeStruct(outer.shape, F32)] * 2,
        scratch_shapes=[pltpu.VMEM((rows, cols), BF16)] * 2
        + [pltpu.VMEM((rows, cols), F32)] * 2
        + [pltpu.SemaphoreType.DMA((4, parts)), pltpu.SemaphoreType.DMA((2, parts))],
        input_output_aliases={4 + i: i for i in range(len(done))},
        compiler_params=pltpu.CompilerParams(vmem_limit_bytes=(44 if done else 32) * 1024 * 1024),
        cost_estimate=pl.CostEstimate(flops=0, bytes_accessed=0, transcendentals=0),
    )(theirs, ours, outer, held, *done)


def piece_kernel(parts, ours, *refs):
    pieces, loads = refs[:-1], refs[-1]
    copies = []
    for (first, cuts), piece in zip(parts, pieces):
        for top, bottom in zip(cuts, cuts[1:]):
            source = ours.at[pl.ds(first + top, bottom - top)]
            copies.append(pltpu.make_async_copy(source, piece.at[pl.ds(top, bottom - top)], loads.at[len(copies)]))
    for copy in copies:
        copy.start()
    for copy in copies:
        copy.wait()


def pieces_of(local_frag, members, hint=0):
    ours = local_frag.reshape(-1, local_frag.shape[-1])
    unit, cols = ours.shape[0] // units, ours.shape[1]
    shapes = [(chunk_units[k][1] * unit, cols) for k in members]
    parts = []
    for k, (rows, _) in zip(members, shapes):
        cuts = list(range(0, rows, 10 * unit)) + [rows]
        parts.append((chunk_units[k][0] * unit, cuts))
    copies = sum(len(cuts) - 1 for _, cuts in parts)
    return pl.pallas_call(
        functools.partial(piece_kernel, parts),
        in_specs=[pl.BlockSpec(memory_space=pltpu.HBM)],
        out_specs=[pl.BlockSpec(memory_space=pltpu.VMEM)] * len(members),
        out_shape=[pltpu.VMEM(s, BF16) if k == 0 else jax.ShapeDtypeStruct(s, BF16) for k, s in zip(members, shapes)],
        scratch_shapes=[pltpu.SemaphoreType.DMA((copies,))],
        compiler_params=pltpu.CompilerParams(vmem_limit_bytes=8 * 1024 * 1024),
        cost_estimate=pl.CostEstimate(flops=hint, bytes_accessed=0, transcendentals=0),
    )(ours)


def swapped(piece):
    return lax.ppermute(piece, "island", [(0, 1), (1, 0)])


def together(f, *operands):
    shapes = jax.eval_shape(f, *operands)
    return lax.cond(
        lax.axis_index("fsdp") >= 0, f, lambda *_: jax.tree.map(lambda s: jnp.zeros(s.shape, s.dtype), shapes), *operands
    )


def shifted(x, axis, step):
    n = lax.axis_size(axis)
    return lax.ppermute(x, axis, [(i, (i + step) % n) for i in range(n)])


def paired(x, axis, bit):
    return lax.ppermute(x, axis, [(i, i ^ bit) for i in range(lax.axis_size(axis))])


def leaving_at(axis, bit):
    return [lax.axis_index(axis) ^ k for k in range(bit, lax.axis_size(axis), 2 * bit)]


def input_terms(cots, weight):
    share = cots.shape[1] // lax.axis_size("tensor")

    def part_of(members):
        rows_of = jnp.concatenate([lax.dynamic_slice_in_dim(cots, m * share, share, 1) for m in members])
        return lax.dot_general(
            rows_of.reshape(-1, cots.shape[2]), weight, (((1,), (1,)), ((), ())), preferred_element_type=F32
        )

    return part_of


def sum_scatter(came, part_of, axis):
    n = lax.axis_size(axis)
    received = {k: [] for k in range(n)}
    bit = 1
    while bit < n:
        leaving = list(range(bit, n, 2 * bit))
        if bit > 1:
            part = part_of(leaving_at(axis, bit))
            for terms in zip(*(received[k] for k in leaving)):
                part = part + jnp.concatenate([t.astype(F32) for t in terms])
            came = paired(part.astype(BF16), axis, bit)
        for slot, block in zip(leaving, jnp.split(came, len(leaving))):
            received[slot ^ bit].append(block)
        bit *= 2
    return part_of([lax.axis_index(axis)]) + sum(t.astype(F32) for t in received[0])


def keys_kernel(place, own, *refs):
    peers = (len(refs) - 3) // 3
    mine, other = refs[:peers], refs[peers : 2 * peers]
    weight, summed, keys_own, *packets = refs[2 * peers :]
    core = place[1]
    half, cols = own.shape[0] // 2, weight.shape[1]
    share = summed.shape[0] // (peers + 1)
    rows = jnp.concatenate([own[...]] + [block[...] for block in (*mine, *other)])
    part = jnp.dot(rows, weight[...], preferred_element_type=F32)
    keys_own[...] = part[: 2 * half]
    part = part.astype(BF16)
    for s, packet in enumerate(packets):
        for top, at in ((2 + s) * half, core), ((2 + peers + s) * half, 1 - core):
            packet[pl.ds(pl.multiple_of(at * half, half), half), :] = part[top : top + half]
    for s, packet in enumerate(packets, 1):
        for j in range(summed.shape[1] // cols):
            top = 2 * half + j * share
            packet[top : top + share, :] = summed[s * share : (s + 1) * share, j * cols : (j + 1) * cols]


def finish_kernel(place, keys_own, summed, *refs):
    packets, (keys, input_grad) = refs[:-2], refs[-2:]
    shards = len(packets) + 1
    rows, cols = keys.shape
    share, width = input_grad.shape[0], summed.shape[1]
    total = keys_own[...]
    for packet in packets:
        total = total + packet[:rows, :].astype(F32)
    keys[...] = total.astype(BF16)
    input_grad[:, pl.ds(pl.multiple_of(place[0] * width, width), width)] = summed[:share, :]
    for s, packet in enumerate(packets, 1):
        origin = lax.rem(place[0] + s, shards) * width
        for j in range(width // cols):
            top = rows + j * share
            input_grad[:, pl.ds(pl.multiple_of(origin + j * cols, cols), cols)] = packet[top : top + share, :]


def weight_grad_kernel(place, own, *refs):
    peers = (len(refs) - 2) // 2
    mine, other, (cots, weight_grad) = refs[:peers], refs[peers : 2 * peers], refs[2 * peers :]
    core = place[1]
    half = own.shape[0] // 2
    tokens, rows = [own[...]], [cots[0]]
    for blocks, at in ((mine, core), (other, 1 - core)):
        for s, block in enumerate(blocks, 1):
            tokens.append(block[...])
            rows.append(cots[s, pl.ds(pl.multiple_of(at * half, half), half), :])
    total = lax.dot_general(
        jnp.concatenate(tokens), jnp.concatenate(rows), (((0,), (0,)), ((), ())), preferred_element_type=F32
    )
    weight_grad[...] = total.astype(BF16)


def local_call(kernel, out_shape, place, tokens, *operands, flops=0):
    whole = pl.BlockSpec(memory_space=pltpu.VMEM)
    first = [] if tokens is None else [tokens]
    width = first[0].shape[1] // lax.axis_size("fsdp") if first else 0
    columns = [pl.BlockSpec((a.shape[0], width), lambda i, place: (0, place[0])) for a in first]
    return pl.pallas_call(
        kernel,
        grid_spec=pltpu.PrefetchScalarGridSpec(
            num_scalar_prefetch=1, grid=(1,), in_specs=columns + [whole] * len(operands), out_specs=[whole] * len(out_shape)
        ),
        out_shape=out_shape,
        compiler_params=pltpu.CompilerParams(vmem_limit_bytes=12 * 1024 * 1024),
        cost_estimate=pl.CostEstimate(flops=flops, bytes_accessed=0, transcendentals=0),
    )(place, *first, *operands)


def place_of():
    return lax.axis_index("fsdp"), lax.rem(lax.axis_index("tensor"), 2)


def columns_for(tokens, s, width):
    me, core = place_of()
    half = tokens.shape[0] // 2
    return lax.dynamic_slice(tokens, (core * half, lax.rem(me + s, lax.axis_size("fsdp")) * width), (half, width))


def gather(tokens, weight, cotangent):
    cots = jnp.stack([cotangent] + [shifted(cotangent, "fsdp", s) for s in range(1, lax.axis_size("fsdp"))])
    part = input_terms(cots, weight)(leaving_at("tensor", 1)).astype(BF16)
    return cots, part, shifted(columns_for(tokens, 1, weight.shape[0]), "fsdp", 1)


def combine(cots, part, mine, tokens, weight):
    place = jnp.stack(place_of()).astype(jnp.int32)
    shards, heads = lax.axis_size("fsdp"), lax.axis_size("tensor")
    width, cols = weight.shape
    rows = tokens.shape[0]
    share = rows // heads

    part = paired(part, "tensor", 1)
    mine = [mine] + [shifted(columns_for(tokens, s, width), "fsdp", s) for s in range(2, shards)]
    other = [paired(block, "tensor", 1) for block in mine]
    summed = sum_scatter(part, input_terms(cots, weight), "tensor").astype(BF16)
    packet = jax.ShapeDtypeStruct((rows + share * width // cols, cols), BF16)
    keys_own, *packets = local_call(
        keys_kernel,
        [jax.ShapeDtypeStruct((rows, cols), F32)] + [packet] * (shards - 1),
        place, tokens, *mine, *other, weight, summed,
    )
    return mine[1:], other, (keys_own, summed), packets


def finish(cots, mine, more, other, own, packets, tokens, weight):
    place = jnp.stack(place_of()).astype(jnp.int32)
    mine = [mine, *more]
    keys_own, summed = own
    shards, rows, cols = cots.shape
    packets = [shifted(p, "fsdp", -s) for s, p in enumerate(packets, 1)]
    (weight_grad,) = local_call(
        weight_grad_kernel, [jax.ShapeDtypeStruct(weight.shape, BF16)], place, tokens, *mine, *other, cots
    )
    keys, input_grad = local_call(
        finish_kernel,
        [jax.ShapeDtypeStruct((rows, cols), BF16), jax.ShapeDtypeStruct((summed.shape[0] // shards, tokens.shape[1]), BF16)],
        place, None, keys_own, summed, *packets,
    )
    return keys, input_grad, weight_grad


def body(tokens, key_weight, key_cotangent, local_frag, outer_frag, momentum):
    weight = key_weight[0]
    islands = lax.axis_size("island")
    if islands != 2:
        cots, part, mine = gather(tokens, weight, key_cotangent)
        state = combine(cots, part, mine, tokens, weight)
        keys, input_grad, weight_grad = finish(cots, mine, *state, tokens, weight)
        frag_sum = lax.psum(local_frag[0], "island").astype(F32)
        new_outer, new_momentum = nesterov(frag_sum, outer_frag, momentum, islands)
        return (keys, input_grad, weight_grad[None], new_outer, new_momentum)

    theirs = [swapped(*pieces_of(local_frag, [0]))]
    cots, part, mine = together(gather, tokens, weight, key_cotangent)

    late = range(2, len(chunk_units))

    def step_two(cots, part, mine, tokens, weight, local_frag):
        return combine(cots, part, mine, tokens, weight), pieces_of(local_frag, range(1, len(chunk_units)), hint=6 * 10**9)

    state, pieces = together(step_two, cots, part, mine, tokens, weight, local_frag)
    theirs += [swapped(piece) for piece in pieces[:-1]]
    theirs[0], state = lax.optimization_barrier((theirs[0], state))

    def step_three(theirs, cots, mine, state, tokens, weight, *frag):
        return finish(cots, mine, *state, tokens, weight), update(0, theirs, *frag, ()), own_terms(late, *frag)

    results, done, terms = together(
        step_three, theirs[0], cots, mine, state, tokens, weight, local_frag, outer_frag, momentum
    )
    keys, input_grad, weight_grad = results
    piece, done = lax.optimization_barrier((pieces[-1], done))
    theirs.append(swapped(piece))
    theirs[1], done = lax.optimization_barrier((theirs[1], done))
    done = update(1, theirs[1], local_frag, outer_frag, momentum, done)
    for k in late:
        theirs[k], done = lax.optimization_barrier((theirs[k], done))
        done = late_update(k, theirs[k], terms, done)
    new_outer, new_momentum = (a.reshape(outer_frag.shape) for a in done)
    return (keys, input_grad, weight_grad[None], new_outer, new_momentum)


def solution(mesh):
    return jax.shard_map(
        body,
        mesh=mesh,
        in_specs=(
            P(("island", "fsdp"), None),
            P("island", "fsdp", "tensor"),
            P(("island", "fsdp"), "tensor"),
            P("island", None, "fsdp", "tensor"),
            P(None, "fsdp", "tensor"),
            P(None, "fsdp", "tensor"),
        ),
        out_specs=(
            P(("island", "fsdp"), "tensor"),
            P(("island", "fsdp", "tensor"), None),
            P("island", "fsdp", "tensor"),
            P(None, "fsdp", "tensor"),
            P(None, "fsdp", "tensor"),
        ),
        check_vma=False,
    )
```

```python
import functools

import jax
import jax.numpy as jnp
from jax import lax
from jax.experimental import pallas as pl
from jax.experimental.pallas import tpu as pltpu
from jax.sharding import PartitionSpec as P

outer_rate = 0.7
beta_outer = 0.9
F32 = jnp.float32
BF16 = jnp.bfloat16
units = 32
late_parts = 2
chunk_units = ((0, 19, 6), (19, 10, 4), (29, 2, None), (31, 1, None))


def nesterov(frag_sum, outer, momentum, islands):
    average = outer - frag_sum / islands
    new_momentum = beta_outer * momentum + average
    return outer - outer_rate * (average + beta_outer * new_momentum), new_momentum


def update_kernel(islands, first, cuts, theirs, ours, outer, momentum, *refs):
    new_outer, new_momentum, their_rows, our_rows, outer_rows, momentum_rows, loads, stores = refs[-8:]
    arriving, leaving = [], []
    for k, (top, bottom) in enumerate(zip(cuts, cuts[1:])):
        here, there = pl.ds(top, bottom - top), pl.ds(first + top, bottom - top)
        sources = (theirs.at[here], ours.at[there], outer.at[there], momentum.at[there])
        buffers = (their_rows, our_rows, outer_rows, momentum_rows)
        arriving.append([pltpu.make_async_copy(s, b.at[here], loads.at[i, k]) for i, (s, b) in enumerate(zip(sources, buffers))])
        results = ((outer_rows, new_outer), (momentum_rows, new_momentum))
        leaving.append([pltpu.make_async_copy(b.at[here], d.at[there], stores.at[i, k]) for i, (b, d) in enumerate(results)])
    for copies in arriving:
        for copy in copies:
            copy.start()
    for (top, bottom), copies, results in zip(zip(cuts, cuts[1:]), arriving, leaving):
        for copy in copies:
            copy.wait()
        rows = slice(top, bottom)
        frag_sum = our_rows[rows].astype(F32) + their_rows[rows].astype(F32)
        outer_rows[rows], momentum_rows[rows] = nesterov(frag_sum, outer_rows[rows], momentum_rows[rows], islands)
        for copy in results:
            copy.start()
    for copies in leaving:
        for copy in copies:
            copy.wait()


def own_terms(late, local_frag, outer_frag, momentum):
    ours, outer, held = (a.reshape(-1, a.shape[-1]) for a in (local_frag, outer_frag, momentum))
    unit = ours.shape[0] // units
    first = chunk_units[late[0]][0]
    last = first + sum(chunk_units[k][1] for k in late)
    ours, outer, held = (lax.slice_in_dim(a, first * unit, last * unit) for a in (ours, outer, held))
    return nesterov(ours.astype(F32), outer, held, lax.axis_size("island"))


def late_kernel(islands, first, skipped, cuts, theirs, outer_terms, momentum_terms, *refs):
    new_outer, new_momentum, outer_rows, momentum_rows, stores = refs[-5:]
    leaving = []
    for k, (top, bottom) in enumerate(zip(cuts, cuts[1:])):
        rows, there = slice(top, bottom), pl.ds(first + top, bottom - top)
        own = slice(skipped + top, skipped + bottom)
        share = theirs[rows].astype(F32) / islands
        outer_rows[rows] = outer_terms[own] + outer_rate * (1 + beta_outer) * share
        momentum_rows[rows] = momentum_terms[own] - share
        for i, (buffer, out) in enumerate(((outer_rows, new_outer), (momentum_rows, new_momentum))):
            leaving.append(pltpu.make_async_copy(buffer.at[pl.ds(top, bottom - top)], out.at[there], stores.at[i, k]))
            leaving[-1].start()
    for copy in leaving:
        copy.wait()


def late_update(k, theirs, terms, done):
    rows, cols = theirs.shape
    first = chunk_units[k][0] * (done[0].shape[0] // units)
    cuts = [rows * i // late_parts // 16 * 16 for i in range(late_parts)] + [rows]
    hbm, vmem = pl.BlockSpec(memory_space=pltpu.HBM), pl.BlockSpec(memory_space=pltpu.VMEM)
    return pl.pallas_call(
        functools.partial(late_kernel, lax.axis_size("island"), first, first - done[0].shape[0] + terms[0].shape[0], cuts),
        in_specs=[vmem] * 3 + [hbm] * 2,
        out_specs=[hbm] * 2,
        out_shape=[jax.ShapeDtypeStruct(a.shape, F32) for a in done],
        scratch_shapes=[pltpu.VMEM((rows, cols), F32)] * 2 + [pltpu.SemaphoreType.DMA((2, late_parts))],
        input_output_aliases={3: 0, 4: 1},
        compiler_params=pltpu.CompilerParams(vmem_limit_bytes=44 * 1024 * 1024),
        cost_estimate=pl.CostEstimate(flops=0, bytes_accessed=0, transcendentals=0),
    )(theirs, *terms, *done)


def update(k, theirs, local_frag, outer_frag, momentum, done):
    islands = lax.axis_size("island")
    ours, outer, held = (a.reshape(-1, a.shape[-1]) for a in (local_frag, outer_frag, momentum))
    unit = ours.shape[0] // units
    (first, size, parts), cols = chunk_units[k], ours.shape[1]
    first, rows = first * unit, size * unit
    cuts = [rows * i // parts // 16 * 16 for i in range(parts)] + [rows]
    hbm = pl.BlockSpec(memory_space=pltpu.HBM)
    return pl.pallas_call(
        functools.partial(update_kernel, islands, first, cuts),
        in_specs=[hbm] * (4 + len(done)),
        out_specs=[hbm] * 2,
        out_shape=[jax.ShapeDtypeStruct(outer.shape, F32)] * 2,
        scratch_shapes=[pltpu.VMEM((rows, cols), BF16)] * 2
        + [pltpu.VMEM((rows, cols), F32)] * 2
        + [pltpu.SemaphoreType.DMA((4, parts)), pltpu.SemaphoreType.DMA((2, parts))],
        input_output_aliases={4 + i: i for i in range(len(done))},
        compiler_params=pltpu.CompilerParams(vmem_limit_bytes=(44 if done else 32) * 1024 * 1024),
        cost_estimate=pl.CostEstimate(flops=0, bytes_accessed=0, transcendentals=0),
    )(theirs, ours, outer, held, *done)


def piece_kernel(parts, ours, *refs):
    pieces, loads = refs[:-1], refs[-1]
    copies = []
    for (first, cuts), piece in zip(parts, pieces):
        for top, bottom in zip(cuts, cuts[1:]):
            source = ours.at[pl.ds(first + top, bottom - top)]
            copies.append(pltpu.make_async_copy(source, piece.at[pl.ds(top, bottom - top)], loads.at[len(copies)]))
    for copy in copies:
        copy.start()
    for copy in copies:
        copy.wait()


def pieces_of(local_frag, members, hint=0):
    ours = local_frag.reshape(-1, local_frag.shape[-1])
    unit, cols = ours.shape[0] // units, ours.shape[1]
    shapes = [(chunk_units[k][1] * unit, cols) for k in members]
    parts = []
    for k, (rows, _) in zip(members, shapes):
        cuts = list(range(0, rows, 10 * unit)) + [rows]
        parts.append((chunk_units[k][0] * unit, cuts))
    copies = sum(len(cuts) - 1 for _, cuts in parts)
    return pl.pallas_call(
        functools.partial(piece_kernel, parts),
        in_specs=[pl.BlockSpec(memory_space=pltpu.HBM)],
        out_specs=[pl.BlockSpec(memory_space=pltpu.VMEM)] * len(members),
        out_shape=[pltpu.VMEM(s, BF16) if k == 0 else jax.ShapeDtypeStruct(s, BF16) for k, s in zip(members, shapes)],
        scratch_shapes=[pltpu.SemaphoreType.DMA((copies,))],
        compiler_params=pltpu.CompilerParams(vmem_limit_bytes=8 * 1024 * 1024),
        cost_estimate=pl.CostEstimate(flops=hint, bytes_accessed=0, transcendentals=0),
    )(ours)


def swapped(piece):
    return lax.ppermute(piece, "island", [(0, 1), (1, 0)])


def together(f, *operands):
    shapes = jax.eval_shape(f, *operands)
    return lax.cond(
        lax.axis_index("fsdp") >= 0, f, lambda *_: jax.tree.map(lambda s: jnp.zeros(s.shape, s.dtype), shapes), *operands
    )


def shifted(x, axis, step):
    n = lax.axis_size(axis)
    return lax.ppermute(x, axis, [(i, (i + step) % n) for i in range(n)])


def paired(x, axis, bit):
    return lax.ppermute(x, axis, [(i, i ^ bit) for i in range(lax.axis_size(axis))])


def leaving_at(axis, bit):
    return [lax.axis_index(axis) ^ k for k in range(bit, lax.axis_size(axis), 2 * bit)]


def input_terms(cots, weight):
    share = cots.shape[1] // lax.axis_size("tensor")

    def part_of(members):
        rows_of = jnp.concatenate([lax.dynamic_slice_in_dim(cots, m * share, share, 1) for m in members])
        return lax.dot_general(
            rows_of.reshape(-1, cots.shape[2]), weight, (((1,), (1,)), ((), ())), preferred_element_type=F32
        )

    return part_of


def sum_scatter(came, part_of, axis):
    n = lax.axis_size(axis)
    received = {k: [] for k in range(n)}
    bit = 1
    while bit < n:
        leaving = list(range(bit, n, 2 * bit))
        if bit > 1:
            part = part_of(leaving_at(axis, bit))
            for terms in zip(*(received[k] for k in leaving)):
                part = part + jnp.concatenate([t.astype(F32) for t in terms])
            came = paired(part.astype(BF16), axis, bit)
        for slot, block in zip(leaving, jnp.split(came, len(leaving))):
            received[slot ^ bit].append(block)
        bit *= 2
    return part_of([lax.axis_index(axis)]) + sum(t.astype(F32) for t in received[0])


def keys_kernel(place, own, *refs):
    peers = (len(refs) - 3) // 3
    mine, other = refs[:peers], refs[peers : 2 * peers]
    weight, summed, keys_own, *packets = refs[2 * peers :]
    core = place[1]
    half, cols = own.shape[0] // 2, weight.shape[1]
    share = summed.shape[0] // (peers + 1)
    rows = jnp.concatenate([own[...]] + [block[...] for block in (*mine, *other)])
    part = jnp.dot(rows, weight[...], preferred_element_type=F32)
    keys_own[...] = part[: 2 * half]
    part = part.astype(BF16)
    for s, packet in enumerate(packets):
        for top, at in ((2 + s) * half, core), ((2 + peers + s) * half, 1 - core):
            packet[pl.ds(pl.multiple_of(at * half, half), half), :] = part[top : top + half]
    for s, packet in enumerate(packets, 1):
        for j in range(summed.shape[1] // cols):
            top = 2 * half + j * share
            packet[top : top + share, :] = summed[s * share : (s + 1) * share, j * cols : (j + 1) * cols]


def finish_kernel(place, keys_own, summed, *refs):
    packets, (keys, input_grad) = refs[:-2], refs[-2:]
    shards = len(packets) + 1
    rows, cols = keys.shape
    share, width = input_grad.shape[0], summed.shape[1]
    total = keys_own[...]
    for packet in packets:
        total = total + packet[:rows, :].astype(F32)
    keys[...] = total.astype(BF16)
    input_grad[:, pl.ds(pl.multiple_of(place[0] * width, width), width)] = summed[:share, :]
    for s, packet in enumerate(packets, 1):
        origin = lax.rem(place[0] + s, shards) * width
        for j in range(width // cols):
            top = rows + j * share
            input_grad[:, pl.ds(pl.multiple_of(origin + j * cols, cols), cols)] = packet[top : top + share, :]


def weight_grad_kernel(place, own, *refs):
    peers = (len(refs) - 2) // 2
    mine, other, (cots, weight_grad) = refs[:peers], refs[peers : 2 * peers], refs[2 * peers :]
    core = place[1]
    half = own.shape[0] // 2
    tokens, rows = [own[...]], [cots[0]]
    for blocks, at in ((mine, core), (other, 1 - core)):
        for s, block in enumerate(blocks, 1):
            tokens.append(block[...])
            rows.append(cots[s, pl.ds(pl.multiple_of(at * half, half), half), :])
    total = lax.dot_general(
        jnp.concatenate(tokens), jnp.concatenate(rows), (((0,), (0,)), ((), ())), preferred_element_type=F32
    )
    weight_grad[...] = total.astype(BF16)


def local_call(kernel, out_shape, place, tokens, *operands, flops=0):
    whole = pl.BlockSpec(memory_space=pltpu.VMEM)
    first = [] if tokens is None else [tokens]
    width = first[0].shape[1] // lax.axis_size("fsdp") if first else 0
    columns = [pl.BlockSpec((a.shape[0], width), lambda i, place: (0, place[0])) for a in first]
    return pl.pallas_call(
        kernel,
        grid_spec=pltpu.PrefetchScalarGridSpec(
            num_scalar_prefetch=1, grid=(1,), in_specs=columns + [whole] * len(operands), out_specs=[whole] * len(out_shape)
        ),
        out_shape=out_shape,
        compiler_params=pltpu.CompilerParams(vmem_limit_bytes=12 * 1024 * 1024),
        cost_estimate=pl.CostEstimate(flops=flops, bytes_accessed=0, transcendentals=0),
    )(place, *first, *operands)


def place_of():
    return lax.axis_index("fsdp"), lax.rem(lax.axis_index("tensor"), 2)


def columns_for(tokens, s, width):
    me, core = place_of()
    half = tokens.shape[0] // 2
    return lax.dynamic_slice(tokens, (core * half, lax.rem(me + s, lax.axis_size("fsdp")) * width), (half, width))


def gather(tokens, weight, cotangent):
    cots = jnp.stack([cotangent] + [shifted(cotangent, "fsdp", s) for s in range(1, lax.axis_size("fsdp"))])
    part = input_terms(cots, weight)(leaving_at("tensor", 1)).astype(BF16)
    return cots, part, shifted(columns_for(tokens, 1, weight.shape[0]), "fsdp", 1)


def combine(cots, part, mine, tokens, weight):
    place = jnp.stack(place_of()).astype(jnp.int32)
    shards, heads = lax.axis_size("fsdp"), lax.axis_size("tensor")
    width, cols = weight.shape
    rows = tokens.shape[0]
    share = rows // heads

    part = paired(part, "tensor", 1)
    mine = [mine] + [shifted(columns_for(tokens, s, width), "fsdp", s) for s in range(2, shards)]
    other = [paired(block, "tensor", 1) for block in mine]
    summed = sum_scatter(part, input_terms(cots, weight), "tensor").astype(BF16)
    packet = jax.ShapeDtypeStruct((rows + share * width // cols, cols), BF16)
    keys_own, *packets = local_call(
        keys_kernel,
        [jax.ShapeDtypeStruct((rows, cols), F32)] + [packet] * (shards - 1),
        place, tokens, *mine, *other, weight, summed,
    )
    return mine[1:], other, (keys_own, summed), packets


def finish(cots, mine, more, other, own, packets, tokens, weight):
    place = jnp.stack(place_of()).astype(jnp.int32)
    mine = [mine, *more]
    keys_own, summed = own
    shards, rows, cols = cots.shape
    packets = [shifted(p, "fsdp", -s) for s, p in enumerate(packets, 1)]
    (weight_grad,) = local_call(
        weight_grad_kernel, [jax.ShapeDtypeStruct(weight.shape, BF16)], place, tokens, *mine, *other, cots
    )
    keys, input_grad = local_call(
        finish_kernel,
        [jax.ShapeDtypeStruct((rows, cols), BF16), jax.ShapeDtypeStruct((summed.shape[0] // shards, tokens.shape[1]), BF16)],
        place, None, keys_own, summed, *packets,
    )
    return keys, input_grad, weight_grad


def body(tokens, key_weight, key_cotangent, local_frag, outer_frag, momentum):
    weight = key_weight[0]
    islands = lax.axis_size("island")
    if islands != 2:
        cots, part, mine = gather(tokens, weight, key_cotangent)
        state = combine(cots, part, mine, tokens, weight)
        keys, input_grad, weight_grad = finish(cots, mine, *state, tokens, weight)
        frag_sum = lax.psum(local_frag[0], "island").astype(F32)
        new_outer, new_momentum = nesterov(frag_sum, outer_frag, momentum, islands)
        return (keys, input_grad, weight_grad[None], new_outer, new_momentum)

    theirs = [swapped(*pieces_of(local_frag, [0]))]
    cots, part, mine = together(gather, tokens, weight, key_cotangent)

    late = range(2, len(chunk_units))

    def step_two(cots, part, mine, tokens, weight, local_frag):
        return combine(cots, part, mine, tokens, weight), pieces_of(local_frag, range(1, len(chunk_units)), hint=6 * 10**9)

    state, pieces = together(step_two, cots, part, mine, tokens, weight, local_frag)
    theirs += [swapped(piece) for piece in pieces[:-1]]
    theirs[0], state = lax.optimization_barrier((theirs[0], state))

    def step_three(theirs, cots, mine, state, tokens, weight, *frag):
        return finish(cots, mine, *state, tokens, weight), update(0, theirs, *frag, ()), own_terms(late, *frag)

    results, done, terms = together(
        step_three, theirs[0], cots, mine, state, tokens, weight, local_frag, outer_frag, momentum
    )
    keys, input_grad, weight_grad = results
    piece, done = lax.optimization_barrier((pieces[-1], done))
    theirs.append(swapped(piece))
    theirs[1], done = lax.optimization_barrier((theirs[1], done))
    done = update(1, theirs[1], local_frag, outer_frag, momentum, done)
    for k in late:
        theirs[k], done = lax.optimization_barrier((theirs[k], done))
        done = late_update(k, theirs[k], terms, done)
    new_outer, new_momentum = (a.reshape(outer_frag.shape) for a in done)
    return (keys, input_grad, weight_grad[None], new_outer, new_momentum)


def solution(mesh):
    return jax.shard_map(
        body,
        mesh=mesh,
        in_specs=(
            P(("island", "fsdp"), None),
            P("island", "fsdp", "tensor"),
            P(("island", "fsdp"), "tensor"),
            P("island", None, "fsdp", "tensor"),
            P(None, "fsdp", "tensor"),
            P(None, "fsdp", "tensor"),
        ),
        out_specs=(
            P(("island", "fsdp"), "tensor"),
            P(("island", "fsdp", "tensor"), None),
            P("island", "fsdp", "tensor"),
            P(None, "fsdp", "tensor"),
            P(None, "fsdp", "tensor"),
        ),
        check_vma=False,
    )
```

```python
import functools

import jax
import jax.numpy as jnp
from jax import lax
from jax.experimental import pallas as pl
from jax.experimental.pallas import tpu as pltpu
from jax.sharding import PartitionSpec as P

outer_rate = 0.7
beta_outer = 0.9
F32 = jnp.float32
BF16 = jnp.bfloat16
units = 32
late_parts = 2
chunk_units = ((0, 19, 6), (19, 10, 4), (29, 2, None), (31, 1, None))


def nesterov(frag_sum, outer, momentum, islands):
    average = outer - frag_sum / islands
    new_momentum = beta_outer * momentum + average
    return outer - outer_rate * (average + beta_outer * new_momentum), new_momentum


def update_kernel(islands, first, cuts, theirs, ours, outer, momentum, *refs):
    new_outer, new_momentum, their_rows, our_rows, outer_rows, momentum_rows, loads, stores = refs[-8:]
    arriving, leaving = [], []
    for k, (top, bottom) in enumerate(zip(cuts, cuts[1:])):
        here, there = pl.ds(top, bottom - top), pl.ds(first + top, bottom - top)
        sources = (theirs.at[here], ours.at[there], outer.at[there], momentum.at[there])
        buffers = (their_rows, our_rows, outer_rows, momentum_rows)
        arriving.append([pltpu.make_async_copy(s, b.at[here], loads.at[i, k]) for i, (s, b) in enumerate(zip(sources, buffers))])
        results = ((outer_rows, new_outer), (momentum_rows, new_momentum))
        leaving.append([pltpu.make_async_copy(b.at[here], d.at[there], stores.at[i, k]) for i, (b, d) in enumerate(results)])
    for copies in arriving:
        for copy in copies:
            copy.start()
    for (top, bottom), copies, results in zip(zip(cuts, cuts[1:]), arriving, leaving):
        for copy in copies:
            copy.wait()
        rows = slice(top, bottom)
        frag_sum = our_rows[rows].astype(F32) + their_rows[rows].astype(F32)
        outer_rows[rows], momentum_rows[rows] = nesterov(frag_sum, outer_rows[rows], momentum_rows[rows], islands)
        for copy in results:
            copy.start()
    for copies in leaving:
        for copy in copies:
            copy.wait()


def own_terms(late, local_frag, outer_frag, momentum):
    ours, outer, held = (a.reshape(-1, a.shape[-1]) for a in (local_frag, outer_frag, momentum))
    unit = ours.shape[0] // units
    first = chunk_units[late[0]][0]
    last = first + sum(chunk_units[k][1] for k in late)
    ours, outer, held = (lax.slice_in_dim(a, first * unit, last * unit) for a in (ours, outer, held))
    return nesterov(ours.astype(F32), outer, held, lax.axis_size("island"))


def late_kernel(islands, first, skipped, cuts, theirs, outer_terms, momentum_terms, *refs):
    new_outer, new_momentum, outer_rows, momentum_rows, stores = refs[-5:]
    leaving = []
    for k, (top, bottom) in enumerate(zip(cuts, cuts[1:])):
        rows, there = slice(top, bottom), pl.ds(first + top, bottom - top)
        own = slice(skipped + top, skipped + bottom)
        share = theirs[rows].astype(F32) / islands
        outer_rows[rows] = outer_terms[own] + outer_rate * (1 + beta_outer) * share
        momentum_rows[rows] = momentum_terms[own] - share
        for i, (buffer, out) in enumerate(((outer_rows, new_outer), (momentum_rows, new_momentum))):
            leaving.append(pltpu.make_async_copy(buffer.at[pl.ds(top, bottom - top)], out.at[there], stores.at[i, k]))
            leaving[-1].start()
    for copy in leaving:
        copy.wait()


def late_update(k, theirs, terms, done):
    rows, cols = theirs.shape
    first = chunk_units[k][0] * (done[0].shape[0] // units)
    cuts = [rows * i // late_parts // 16 * 16 for i in range(late_parts)] + [rows]
    hbm, vmem = pl.BlockSpec(memory_space=pltpu.HBM), pl.BlockSpec(memory_space=pltpu.VMEM)
    return pl.pallas_call(
        functools.partial(late_kernel, lax.axis_size("island"), first, first - done[0].shape[0] + terms[0].shape[0], cuts),
        in_specs=[vmem] * 3 + [hbm] * 2,
        out_specs=[hbm] * 2,
        out_shape=[jax.ShapeDtypeStruct(a.shape, F32) for a in done],
        scratch_shapes=[pltpu.VMEM((rows, cols), F32)] * 2 + [pltpu.SemaphoreType.DMA((2, late_parts))],
        input_output_aliases={3: 0, 4: 1},
        compiler_params=pltpu.CompilerParams(vmem_limit_bytes=44 * 1024 * 1024),
        cost_estimate=pl.CostEstimate(flops=0, bytes_accessed=0, transcendentals=0),
    )(theirs, *terms, *done)


def update(k, theirs, local_frag, outer_frag, momentum, done):
    islands = lax.axis_size("island")
    ours, outer, held = (a.reshape(-1, a.shape[-1]) for a in (local_frag, outer_frag, momentum))
    unit = ours.shape[0] // units
    (first, size, parts), cols = chunk_units[k], ours.shape[1]
    first, rows = first * unit, size * unit
    cuts = [rows * i // parts // 16 * 16 for i in range(parts)] + [rows]
    hbm = pl.BlockSpec(memory_space=pltpu.HBM)
    return pl.pallas_call(
        functools.partial(update_kernel, islands, first, cuts),
        in_specs=[hbm] * (4 + len(done)),
        out_specs=[hbm] * 2,
        out_shape=[jax.ShapeDtypeStruct(outer.shape, F32)] * 2,
        scratch_shapes=[pltpu.VMEM((rows, cols), BF16)] * 2
        + [pltpu.VMEM((rows, cols), F32)] * 2
        + [pltpu.SemaphoreType.DMA((4, parts)), pltpu.SemaphoreType.DMA((2, parts))],
        input_output_aliases={4 + i: i for i in range(len(done))},
        compiler_params=pltpu.CompilerParams(vmem_limit_bytes=(44 if done else 32) * 1024 * 1024),
        cost_estimate=pl.CostEstimate(flops=0, bytes_accessed=0, transcendentals=0),
    )(theirs, ours, outer, held, *done)


def piece_kernel(parts, ours, *refs):
    pieces, loads = refs[:-1], refs[-1]
    copies = []
    for (first, cuts), piece in zip(parts, pieces):
        for top, bottom in zip(cuts, cuts[1:]):
            source = ours.at[pl.ds(first + top, bottom - top)]
            copies.append(pltpu.make_async_copy(source, piece.at[pl.ds(top, bottom - top)], loads.at[len(copies)]))
    for copy in copies:
        copy.start()
    for copy in copies:
        copy.wait()


def pieces_of(local_frag, members, hint=0):
    ours = local_frag.reshape(-1, local_frag.shape[-1])
    unit, cols = ours.shape[0] // units, ours.shape[1]
    shapes = [(chunk_units[k][1] * unit, cols) for k in members]
    parts = []
    for k, (rows, _) in zip(members, shapes):
        cuts = list(range(0, rows, 7 * unit)) + [rows]
        parts.append((chunk_units[k][0] * unit, cuts))
    copies = sum(len(cuts) - 1 for _, cuts in parts)
    return pl.pallas_call(
        functools.partial(piece_kernel, parts),
        in_specs=[pl.BlockSpec(memory_space=pltpu.HBM)],
        out_specs=[pl.BlockSpec(memory_space=pltpu.VMEM)] * len(members),
        out_shape=[pltpu.VMEM(s, BF16) if k == 0 else jax.ShapeDtypeStruct(s, BF16) for k, s in zip(members, shapes)],
        scratch_shapes=[pltpu.SemaphoreType.DMA((copies,))],
        compiler_params=pltpu.CompilerParams(vmem_limit_bytes=8 * 1024 * 1024),
        cost_estimate=pl.CostEstimate(flops=hint, bytes_accessed=0, transcendentals=0),
    )(ours)


def swapped(piece):
    return lax.ppermute(piece, "island", [(0, 1), (1, 0)])


def together(f, *operands):
    shapes = jax.eval_shape(f, *operands)
    return lax.cond(
        lax.axis_index("fsdp") >= 0, f, lambda *_: jax.tree.map(lambda s: jnp.zeros(s.shape, s.dtype), shapes), *operands
    )


def shifted(x, axis, step):
    n = lax.axis_size(axis)
    return lax.ppermute(x, axis, [(i, (i + step) % n) for i in range(n)])


def paired(x, axis, bit):
    return lax.ppermute(x, axis, [(i, i ^ bit) for i in range(lax.axis_size(axis))])


def leaving_at(axis, bit):
    return [lax.axis_index(axis) ^ k for k in range(bit, lax.axis_size(axis), 2 * bit)]


def input_terms(cots, weight):
    share = cots.shape[1] // lax.axis_size("tensor")

    def part_of(members):
        rows_of = jnp.concatenate([lax.dynamic_slice_in_dim(cots, m * share, share, 1) for m in members])
        return lax.dot_general(
            rows_of.reshape(-1, cots.shape[2]), weight, (((1,), (1,)), ((), ())), preferred_element_type=F32
        )

    return part_of


def sum_scatter(came, part_of, axis):
    n = lax.axis_size(axis)
    received = {k: [] for k in range(n)}
    bit = 1
    while bit < n:
        leaving = list(range(bit, n, 2 * bit))
        if bit > 1:
            part = part_of(leaving_at(axis, bit))
            for terms in zip(*(received[k] for k in leaving)):
                part = part + jnp.concatenate([t.astype(F32) for t in terms])
            came = paired(part.astype(BF16), axis, bit)
        for slot, block in zip(leaving, jnp.split(came, len(leaving))):
            received[slot ^ bit].append(block)
        bit *= 2
    return part_of([lax.axis_index(axis)]) + sum(t.astype(F32) for t in received[0])


def keys_kernel(place, own, *refs):
    peers = (len(refs) - 3) // 3
    mine, other = refs[:peers], refs[peers : 2 * peers]
    weight, summed, keys_own, *packets = refs[2 * peers :]
    core = place[1]
    half, cols = own.shape[0] // 2, weight.shape[1]
    share = summed.shape[0] // (peers + 1)
    rows = jnp.concatenate([own[...]] + [block[...] for block in (*mine, *other)])
    part = jnp.dot(rows, weight[...], preferred_element_type=F32)
    keys_own[...] = part[: 2 * half]
    part = part.astype(BF16)
    for s, packet in enumerate(packets):
        for top, at in ((2 + s) * half, core), ((2 + peers + s) * half, 1 - core):
            packet[pl.ds(pl.multiple_of(at * half, half), half), :] = part[top : top + half]
    for s, packet in enumerate(packets, 1):
        for j in range(summed.shape[1] // cols):
            top = 2 * half + j * share
            packet[top : top + share, :] = summed[s * share : (s + 1) * share, j * cols : (j + 1) * cols]


def finish_kernel(place, keys_own, summed, *refs):
    packets, (keys, input_grad) = refs[:-2], refs[-2:]
    shards = len(packets) + 1
    rows, cols = keys.shape
    share, width = input_grad.shape[0], summed.shape[1]
    total = keys_own[...]
    for packet in packets:
        total = total + packet[:rows, :].astype(F32)
    keys[...] = total.astype(BF16)
    input_grad[:, pl.ds(pl.multiple_of(place[0] * width, width), width)] = summed[:share, :]
    for s, packet in enumerate(packets, 1):
        origin = lax.rem(place[0] + s, shards) * width
        for j in range(width // cols):
            top = rows + j * share
            input_grad[:, pl.ds(pl.multiple_of(origin + j * cols, cols), cols)] = packet[top : top + share, :]


def weight_grad_kernel(place, own, *refs):
    peers = (len(refs) - 2) // 2
    mine, other, (cots, weight_grad) = refs[:peers], refs[peers : 2 * peers], refs[2 * peers :]
    core = place[1]
    half = own.shape[0] // 2
    tokens, rows = [own[...]], [cots[0]]
    for blocks, at in ((mine, core), (other, 1 - core)):
        for s, block in enumerate(blocks, 1):
            tokens.append(block[...])
            rows.append(cots[s, pl.ds(pl.multiple_of(at * half, half), half), :])
    total = lax.dot_general(
        jnp.concatenate(tokens), jnp.concatenate(rows), (((0,), (0,)), ((), ())), preferred_element_type=F32
    )
    weight_grad[...] = total.astype(BF16)


def local_call(kernel, out_shape, place, tokens, *operands, flops=0):
    whole = pl.BlockSpec(memory_space=pltpu.VMEM)
    first = [] if tokens is None else [tokens]
    width = first[0].shape[1] // lax.axis_size("fsdp") if first else 0
    columns = [pl.BlockSpec((a.shape[0], width), lambda i, place: (0, place[0])) for a in first]
    return pl.pallas_call(
        kernel,
        grid_spec=pltpu.PrefetchScalarGridSpec(
            num_scalar_prefetch=1, grid=(1,), in_specs=columns + [whole] * len(operands), out_specs=[whole] * len(out_shape)
        ),
        out_shape=out_shape,
        compiler_params=pltpu.CompilerParams(vmem_limit_bytes=12 * 1024 * 1024),
        cost_estimate=pl.CostEstimate(flops=flops, bytes_accessed=0, transcendentals=0),
    )(place, *first, *operands)


def place_of():
    return lax.axis_index("fsdp"), lax.rem(lax.axis_index("tensor"), 2)


def columns_for(tokens, s, width):
    me, core = place_of()
    half = tokens.shape[0] // 2
    return lax.dynamic_slice(tokens, (core * half, lax.rem(me + s, lax.axis_size("fsdp")) * width), (half, width))


def gather(tokens, weight, cotangent):
    cots = jnp.stack([cotangent] + [shifted(cotangent, "fsdp", s) for s in range(1, lax.axis_size("fsdp"))])
    part = input_terms(cots, weight)(leaving_at("tensor", 1)).astype(BF16)
    return cots, part, shifted(columns_for(tokens, 1, weight.shape[0]), "fsdp", 1)


def combine(cots, part, mine, tokens, weight):
    place = jnp.stack(place_of()).astype(jnp.int32)
    shards, heads = lax.axis_size("fsdp"), lax.axis_size("tensor")
    width, cols = weight.shape
    rows = tokens.shape[0]
    share = rows // heads

    part = paired(part, "tensor", 1)
    mine = [mine] + [shifted(columns_for(tokens, s, width), "fsdp", s) for s in range(2, shards)]
    other = [paired(block, "tensor", 1) for block in mine]
    summed = sum_scatter(part, input_terms(cots, weight), "tensor").astype(BF16)
    packet = jax.ShapeDtypeStruct((rows + share * width // cols, cols), BF16)
    keys_own, *packets = local_call(
        keys_kernel,
        [jax.ShapeDtypeStruct((rows, cols), F32)] + [packet] * (shards - 1),
        place, tokens, *mine, *other, weight, summed,
    )
    return mine[1:], other, (keys_own, summed), packets


def finish(cots, mine, more, other, own, packets, tokens, weight):
    place = jnp.stack(place_of()).astype(jnp.int32)
    mine = [mine, *more]
    keys_own, summed = own
    shards, rows, cols = cots.shape
    packets = [shifted(p, "fsdp", -s) for s, p in enumerate(packets, 1)]
    (weight_grad,) = local_call(
        weight_grad_kernel, [jax.ShapeDtypeStruct(weight.shape, BF16)], place, tokens, *mine, *other, cots
    )
    keys, input_grad = local_call(
        finish_kernel,
        [jax.ShapeDtypeStruct((rows, cols), BF16), jax.ShapeDtypeStruct((summed.shape[0] // shards, tokens.shape[1]), BF16)],
        place, None, keys_own, summed, *packets,
    )
    return keys, input_grad, weight_grad


def body(tokens, key_weight, key_cotangent, local_frag, outer_frag, momentum):
    weight = key_weight[0]
    islands = lax.axis_size("island")
    if islands != 2:
        cots, part, mine = gather(tokens, weight, key_cotangent)
        state = combine(cots, part, mine, tokens, weight)
        keys, input_grad, weight_grad = finish(cots, mine, *state, tokens, weight)
        frag_sum = lax.psum(local_frag[0], "island").astype(F32)
        new_outer, new_momentum = nesterov(frag_sum, outer_frag, momentum, islands)
        return (keys, input_grad, weight_grad[None], new_outer, new_momentum)

    theirs = [swapped(*pieces_of(local_frag, [0]))]
    cots, part, mine = together(gather, tokens, weight, key_cotangent)

    late = range(2, len(chunk_units))

    def step_two(cots, part, mine, tokens, weight, local_frag):
        return combine(cots, part, mine, tokens, weight), pieces_of(local_frag, range(1, len(chunk_units)), hint=6 * 10**9)

    state, pieces = together(step_two, cots, part, mine, tokens, weight, local_frag)
    theirs += [swapped(piece) for piece in pieces[:-1]]
    theirs[0], state = lax.optimization_barrier((theirs[0], state))

    def step_three(theirs, cots, mine, state, tokens, weight, *frag):
        return finish(cots, mine, *state, tokens, weight), update(0, theirs, *frag, ()), own_terms(late, *frag)

    results, done, terms = together(
        step_three, theirs[0], cots, mine, state, tokens, weight, local_frag, outer_frag, momentum
    )
    keys, input_grad, weight_grad = results
    piece, done = lax.optimization_barrier((pieces[-1], done))
    theirs.append(swapped(piece))
    theirs[1], done = lax.optimization_barrier((theirs[1], done))
    done = update(1, theirs[1], local_frag, outer_frag, momentum, done)
    for k in late:
        theirs[k], done = lax.optimization_barrier((theirs[k], done))
        done = late_update(k, theirs[k], terms, done)
    new_outer, new_momentum = (a.reshape(outer_frag.shape) for a in done)
    return (keys, input_grad, weight_grad[None], new_outer, new_momentum)


def solution(mesh):
    return jax.shard_map(
        body,
        mesh=mesh,
        in_specs=(
            P(("island", "fsdp"), None),
            P("island", "fsdp", "tensor"),
            P(("island", "fsdp"), "tensor"),
            P("island", None, "fsdp", "tensor"),
            P(None, "fsdp", "tensor"),
            P(None, "fsdp", "tensor"),
        ),
        out_specs=(
            P(("island", "fsdp"), "tensor"),
            P(("island", "fsdp", "tensor"), None),
            P("island", "fsdp", "tensor"),
            P(None, "fsdp", "tensor"),
            P(None, "fsdp", "tensor"),
        ),
        check_vma=False,
    )
```
